32 devices in a mesh: dp: 4 (over z), expert: 8 (over y, x, core).
Axes of the slice: x: 2, y: 2, z: 4, core: 2. Of those that a mesh axis runs over, the one named last changes fastest.
Arguments:
- tokens: bfloat16 [4096, 1024], P(('dp', 'expert')), may hold values from -6 to 6
- grad_out: bfloat16 [4096, 1024], P(('dp', 'expert')), may hold values from -6 to 6
- routes: int32 [4096, 10], P(('dp', 'expert')), may hold values from 0 to 23, all different within a row; in each aligned block of 128 rows (0 to 127, 128 to 255, ...) at most 64 rows name the same one
- combine: bfloat16 [4096, 10], P(('dp', 'expert')), may hold values from 0.049804688 to 0.29882812
- w_gate: bfloat16 [24, 1024, 512], P('expert'), may hold values from -0.1875 to 0.1875
- w_up: bfloat16 [24, 1024, 512], P('expert'), may hold values from -0.1875 to 0.1875
- w_down: bfloat16 [24, 512, 1024], P('expert'), may hold values from -0.25 to 0.25
Outputs:
- grad_tokens: bfloat16 [4096, 1024], P(('dp', 'expert'))
- grad_gate: bfloat16 [24, 1024, 512], P('expert', 'dp')
- grad_up: bfloat16 [24, 1024, 512], P('expert', 'dp')
- grad_down: bfloat16 [24, 512, 1024], P('expert', 'dp')
The draws below stay inside these ranges and needn't reach their ends.
Inputs may be any that keep to these rules, and one draw needn't show every extreme that they name: `routes`: A token's 10 experts are different. Among the 128 tokens of one device no expert is named more than 64 times, a bound that some block reaches.
All inputs are finite; a program needn't handle non-finite values.
Results may differ from the reference program's by a relative error of at most 0.022.
Values may be sent and summed in bfloat16 or wider, within the bound.
No kernel may reach another device: no remote copies, remote signals or barrier semaphores. Data moves between devices by JAX's collectives and lax.ppermute only.
A program may use at most 128 MiB of HBM per device.

```python
import math
import jax
import jax.numpy as jnp
import numpy as np
from jax import lax

D = 1024
FF = 512
TOP = 10
TOK_DEV = 128
EXPERTS = 24
CAP = 64
TOKENS = 4096
N_DP = 4


def shard_levels(own_key, dims, cuts, least, high):
    level = 1.0
    for position, parts in cuts:
        draws = jax.random.uniform(jax.random.fold_in(jax.random.fold_in(own_key, 6), position), (parts,), jnp.float32, least / len(cuts), high / len(cuts))
        level = level * jnp.repeat(jnp.exp(draws), dims[position] // parts).reshape((-1,) + (1,) * (len(dims) - 1 - position))
    return level


def deal_out(own_key, own, number, rows, number_of, top, most, skew):
    ranking = jax.random.permutation(own_key, number_of)
    crowded, usual = shares(number_of, rows * top, most, skew, True), shares(number_of, rows * top, most, skew, False)
    places = jnp.arange(number_of)

    def named(lengths, offset_by):
        used = int((lengths > 0).sum())
        fixed = max(1, used // 4)
        moved = fixed + (places - fixed + offset_by * (used - fixed)) % max(1, number_of - fixed)
        return jnp.zeros((number_of,), jnp.int32).at[ranking[jnp.where(places < fixed, places, moved)]].set(jnp.asarray(lengths, jnp.int32))

    lengths = jnp.where(number % 4 == 0, named(crowded, number // 4), named(usual, number - number // 4 - 1))
    mixed = jax.random.permutation(jax.random.fold_in(own, 3), number_of)
    giver, receiver = mixed[0:number_of // 2 * 2:2], mixed[1:number_of // 2 * 2:2]
    slack = jnp.minimum(lengths[giver] - 1, most - lengths[receiver]) // 2
    slack = jnp.where((giver == ranking[0]) | (receiver == ranking[0]) | (lengths[receiver] == 0), 0, jnp.maximum(slack, 0))
    moved = jax.random.randint(jax.random.fold_in(own, 4), (number_of // 2,), 0, 1 << 20) % (slack + 1)
    lengths = lengths.at[giver].add(-moved).at[receiver].add(moved)
    members = jnp.searchsorted(jnp.cumsum(lengths), jnp.arange(rows * top), side="right").astype(jnp.int32)
    grid = members.reshape(top, rows).T
    grid = grid[jax.random.permutation(jax.random.fold_in(own, 1), rows)]
    offset_by = jax.random.randint(jax.random.fold_in(own, 2), (rows, 1), 0, top)
    return jnp.take_along_axis(grid, (jnp.arange(top)[None, :] + offset_by) % top, axis=1)


def shares(number_of, total, most, slope, full):
    loads = [(1 << 20) // math.isqrt(grade ** slope) + 1 for grade in range(1, number_of + 1)]
    largest = most if full else min(most, max(-(-total // number_of), total * loads[0] // sum(loads)))
    least = 1 if total - largest >= number_of - 1 else 0
    given, rest = [largest] + [least] * (number_of - 1), total - largest - least * (number_of - 1)
    while rest > 0:
        free = [i for i in range(1, number_of) if given[i] < largest] or [i for i in range(1, number_of) if given[i] < most]
        pool, budget = sum([loads[i] for i in free]), rest
        for i in free:
            more = min(most - given[i], max(1, budget * loads[i] // pool), rest)
            given[i] = given[i] + more
            rest = rest - more
    return np.array(given)


def normal_values(own_key, extent, scale, limit, cuts=(), held_as=jnp.bfloat16):
    level = shard_levels(own_key, extent, cuts, -0.22, 0.18) if cuts else 1.0
    result = jax.random.normal(own_key, extent, jnp.float32) * scale * level
    return jnp.minimum(jnp.maximum(result, -limit), limit).astype(held_as)


def setup_inputs(seed: int = 0) -> dict:
    arg_keys = jax.random.split(jax.random.key(seed), 8)
    tokens = normal_values(arg_keys[0], (TOKENS, D), 1.0, 6.0, ((0, 32),))
    grad_out = normal_values(arg_keys[1], (TOKENS, D), 1.0, 6.0, ((0, 32),))
    routes_keys = jax.random.split(jax.random.fold_in(arg_keys[2], 1), TOKENS // TOK_DEV)
    routes_turns = jax.random.permutation(jax.random.fold_in(arg_keys[2], 3), TOKENS // TOK_DEV)
    routes = jax.vmap(lambda own, number: deal_out(jax.random.fold_in(arg_keys[2], 2), own, number, TOK_DEV, EXPERTS, TOP, CAP, 2))(routes_keys, routes_turns).reshape((TOKENS, TOP))
    combine = jnp.clip(0.049804688 + 0.24902344 * jax.random.uniform(arg_keys[3], (TOKENS, TOP), jnp.float32) ** shard_levels(arg_keys[3], (TOKENS, TOP), ((0, 32),), -0.2, 0.2), 0.049804688, 0.29882812).astype(jnp.bfloat16)
    w_gate = normal_values(arg_keys[4], (EXPERTS, D, FF), D ** -0.5, 0.1875, ((0, 8),))
    w_up = normal_values(arg_keys[5], (EXPERTS, D, FF), D ** -0.5, 0.1875, ((0, 8),))
    w_down = normal_values(arg_keys[6], (EXPERTS, FF, D), FF ** -0.5, 0.25, ((0, 8),))
    return dict(tokens=tokens, grad_out=grad_out, routes=routes, combine=combine, w_gate=w_gate, w_up=w_up, w_down=w_down)


def slot_ranks(route_block, expert_total):
    flat_ids = route_block.reshape(-1)
    marks = (flat_ids[:, None] == jnp.arange(expert_total, dtype=jnp.int32)[None, :]).astype(jnp.int32)
    return jnp.sum((jnp.cumsum(marks, axis=0) - 1) * marks, axis=1).astype(jnp.int32)


def build_slots(route_block, expert_total, slot_depth):
    flat_ids = route_block.reshape(-1)
    pair_total = flat_ids.shape[0]
    slot_rank = slot_ranks(route_block, expert_total)
    slots = jnp.full((expert_total, slot_depth), pair_total, dtype=jnp.int32)
    slots = slots.at[flat_ids, slot_rank].set(jnp.arange(pair_total, dtype=jnp.int32))
    return slots, slot_rank


def contract_last(left, right):
    return lax.dot_general(left, right, (((1,), (1,)), ((), ())), preferred_element_type=jnp.float32)


def contract_first(left, right):
    return lax.dot_general(left, right, (((0,), (0,)), ((), ())), preferred_element_type=jnp.float32)


def group_sum(left, right):
    def add_group(total, pieces):
        partial_term = contract_first(pieces[0], pieces[1]).astype(jnp.bfloat16)
        partial_term = lax.optimization_barrier(partial_term)
        return total + partial_term.astype(jnp.float32), None

    start = jnp.zeros((left.shape[2], right.shape[2]), jnp.float32)
    total, unused = lax.scan(add_group, start, (left, right))
    return total.astype(jnp.bfloat16)


def expert_backward(rows_x, rows_dy, rows_c, gate_w, up_w, down_w):
    gate_pre = jnp.dot(rows_x, gate_w, preferred_element_type=jnp.float32)
    up_pre = jnp.dot(rows_x, up_w, preferred_element_type=jnp.float32)
    sigmoid_gate = jax.nn.sigmoid(gate_pre)
    hidden = (gate_pre * sigmoid_gate * up_pre).astype(jnp.bfloat16)
    d_out = (rows_c[:, None] * rows_dy.astype(jnp.float32)).astype(jnp.bfloat16)
    d_hidden = contract_last(d_out, down_w)
    d_gate = (d_hidden * up_pre * sigmoid_gate * (1.0 + gate_pre * (1.0 - sigmoid_gate))).astype(jnp.bfloat16)
    d_up = (d_hidden * gate_pre * sigmoid_gate).astype(jnp.bfloat16)
    d_rows = (contract_last(d_gate, gate_w) + contract_last(d_up, up_w)).astype(jnp.bfloat16)
    return hidden, d_out, d_gate, d_up, d_rows


def reference(tokens, grad_out, routes, combine, w_gate, w_up, w_down):
    sources = TOKENS // TOK_DEV
    pair_total = TOK_DEV * TOP
    blocks = routes.reshape(sources, TOK_DEV, TOP)
    slots, slot_rank = jax.vmap(lambda route_block: build_slots(route_block, EXPERTS, CAP))(blocks)
    filled = slots < pair_total
    pair_base = (jnp.arange(sources, dtype=jnp.int32) * pair_total)[:, None, None]
    global_pair = jnp.where(filled, slots + pair_base, 0).astype(jnp.int32)
    weight_flat = combine.reshape(-1).astype(jnp.float32)

    def one_expert(grad_accum, expert_index):
        is_live = filled[:, expert_index, :].reshape(-1)
        pair_index = global_pair[:, expert_index, :].reshape(-1)
        token_index = (pair_index // TOP).astype(jnp.int32)
        rows_x = jnp.where(is_live[:, None], tokens[token_index], jnp.zeros((), jnp.bfloat16))
        rows_dy = jnp.where(is_live[:, None], grad_out[token_index], jnp.zeros((), jnp.bfloat16))
        rows_c = jnp.where(is_live, weight_flat[pair_index], jnp.zeros((), jnp.float32))
        hidden, d_out, d_gate, d_up, d_rows = expert_backward(
            rows_x, rows_dy, rows_c, w_gate[expert_index], w_up[expert_index], w_down[expert_index])
        added = jnp.where(is_live[:, None], d_rows.astype(jnp.float32), jnp.zeros((), jnp.float32))
        grad_accum = grad_accum.at[token_index].add(added)
        x_groups = rows_x.reshape(N_DP, -1, D)
        grad_g = group_sum(x_groups, d_gate.reshape(N_DP, -1, FF))
        grad_u = group_sum(x_groups, d_up.reshape(N_DP, -1, FF))
        grad_d = group_sum(hidden.reshape(N_DP, -1, FF), d_out.reshape(N_DP, -1, D))
        return grad_accum, (grad_g, grad_u, grad_d)

    start_accum = jnp.zeros((TOKENS, D), jnp.float32)
    totals, grads = lax.scan(one_expert, start_accum, jnp.arange(EXPERTS, dtype=jnp.int32))
    return totals.astype(jnp.bfloat16), grads[0], grads[1], grads[2]
```

```python
import functools
import jax
import jax.numpy as jnp
from jax import lax
from jax.experimental import pallas as pl
from jax.experimental.pallas import tpu as pltpu
from jax.sharding import PartitionSpec as P

LANES = 128
VMEM_BYTES = 60 * 1024 * 1024
GATHER_BYTES = 48 * 1024 * 1024


def slot_ranks(route_block, expert_total):
    flat_ids = route_block.reshape(-1)
    marks = (flat_ids[:, None] == jnp.arange(expert_total, dtype=jnp.int32)[None, :]).astype(
        jnp.int32
    )
    return jnp.sum((jnp.cumsum(marks, axis=0) - 1) * marks, axis=1)


def build_slots(route_block, expert_total, slot_depth):
    flat_ids = route_block.reshape(-1)
    pair_total = flat_ids.shape[0]
    slot_rank = slot_ranks(route_block, expert_total)
    slots = jnp.full((expert_total, slot_depth), pair_total, dtype=jnp.int32)
    slots = slots.at[flat_ids, slot_rank].set(jnp.arange(pair_total, dtype=jnp.int32))
    return (slots, slot_rank)


def contract_last(left, right):
    return lax.dot_general(
        left, right, (((1,), (1,)), ((), ())), preferred_element_type=jnp.float32
    )


def contract_first(left, right):
    return lax.dot_general(
        left, right, (((0,), (0,)), ((), ())), preferred_element_type=jnp.float32
    )


def mul(left, right):
    return jnp.dot(left, right, preferred_element_type=jnp.float32)


def depth_of(tok_dev, top_count, expert_total):
    return 8 * ((tok_dev * top_count * 6 // (5 * expert_total) + 7) // 8)


def expert_backward(rows_x, rows_dy, rows_c, gate_w, up_w, down_w):
    gate_pre = mul(rows_x, gate_w)
    up_pre = mul(rows_x, up_w)
    sigmoid_gate = jax.nn.sigmoid(gate_pre)
    hidden = (gate_pre * sigmoid_gate * up_pre).astype(jnp.bfloat16)
    d_out = (rows_c[:, None] * rows_dy.astype(jnp.float32)).astype(jnp.bfloat16)
    d_hidden = contract_last(d_out, down_w)
    d_gate = (d_hidden * up_pre * sigmoid_gate * (1.0 + gate_pre * (1.0 - sigmoid_gate))).astype(
        jnp.bfloat16
    )
    d_up = (d_hidden * gate_pre * sigmoid_gate).astype(jnp.bfloat16)
    d_rows = (contract_last(d_gate, gate_w) + contract_last(d_up, up_w)).astype(jnp.bfloat16)
    return (hidden, d_out, d_gate, d_up, d_rows)


def routed_shards(tokens, grad_out, routes, combine, w_gate, w_up, w_down):
    tok_dev, model_width = tokens.shape
    top_count = routes.shape[1]
    peer_count = lax.axis_size("expert")
    held_experts = w_gate.shape[0]
    hidden_units = w_gate.shape[2]
    expert_total = peer_count * held_experts
    slot_depth = depth_of(tok_dev, top_count, expert_total)
    pair_total = tok_dev * top_count
    slots, slot_rank = build_slots(routes, expert_total, slot_depth)
    filled = slots < pair_total
    token_index = jnp.where(filled, slots // top_count, tok_dev)
    pad_row = jnp.zeros((1, model_width), jnp.bfloat16)
    send_x = jnp.concatenate([tokens, pad_row])[token_index].reshape(
        peer_count, held_experts, slot_depth, model_width
    )
    send_dy = jnp.concatenate([grad_out, pad_row])[token_index].reshape(
        peer_count, held_experts, slot_depth, model_width
    )
    weight_ext = jnp.concatenate([combine.reshape(-1), jnp.zeros((1,), jnp.bfloat16)])
    send_c = weight_ext[slots].reshape(peer_count, held_experts, slot_depth)
    recv_x, recv_dy, recv_c = (
        lax.all_to_all(send_x, "expert", split_axis=0, concat_axis=0, tiled=True),
        lax.all_to_all(send_dy, "expert", split_axis=0, concat_axis=0, tiled=True),
        lax.all_to_all(send_c, "expert", split_axis=0, concat_axis=0, tiled=True),
    )
    gate_parts = []
    up_parts = []
    down_parts = []
    row_list = []
    for which in range(held_experts):
        rows_x = recv_x[:, which].reshape(-1, model_width)
        rows_dy = recv_dy[:, which].reshape(-1, model_width)
        rows_c = recv_c[:, which].reshape(-1).astype(jnp.float32)
        hidden, d_out, d_gate, d_up, d_rows = expert_backward(
            rows_x, rows_dy, rows_c, w_gate[which], w_up[which], w_down[which]
        )
        d_both = jnp.concatenate([d_gate, d_up], axis=1)
        row_list.append(d_rows.reshape(peer_count, slot_depth, model_width))
        summed = lax.psum_scatter(
            contract_first(rows_x, d_both).astype(jnp.bfloat16),
            "dp",
            scatter_dimension=0,
            tiled=True,
        ).astype(jnp.float32)
        gate_parts.append(summed[:, :hidden_units].astype(jnp.bfloat16))
        up_parts.append(summed[:, hidden_units:].astype(jnp.bfloat16))
        down_parts.append(
            lax.psum_scatter(
                contract_first(hidden, d_out).astype(jnp.bfloat16),
                "dp",
                scatter_dimension=0,
                tiled=True,
            )
        )
    grad_gate = jnp.stack(gate_parts)
    grad_up = jnp.stack(up_parts)
    grad_down = jnp.stack(down_parts)
    stacked = jnp.stack(row_list, axis=1)
    returned = lax.all_to_all(stacked, "expert", split_axis=0, concat_axis=0, tiled=True)
    flat_back = returned.reshape(expert_total * slot_depth, model_width)
    row_of_pair = routes.reshape(-1) * slot_depth + slot_rank
    per_pair = flat_back[row_of_pair].astype(jnp.float32).reshape(tok_dev, top_count, model_width)
    grad_tokens = jnp.sum(per_pair, axis=1).astype(jnp.bfloat16)
    return (grad_tokens, grad_gate, grad_up, grad_down)


def pack_kernel(tok_ref, dy_ref, routes_ref, combine_ref, out_ref):
    tok_dev, width = tok_ref.shape
    half = tok_dev // 2
    out_ref[:, :width] = tok_ref[...]
    out_ref[:, width : 2 * width] = dy_ref[...]
    ids = lax.broadcasted_iota(jnp.int32, (half, tok_dev), 0)
    weight = jnp.zeros((half, tok_dev), jnp.float32)
    named = jnp.zeros((half, tok_dev), jnp.float32)
    for k in range(routes_ref.shape[0]):
        hit = routes_ref[k : k + 1, :] == ids
        weight = jnp.where(hit, combine_ref[k : k + 1, :].astype(jnp.float32), weight)
        named = jnp.where(hit, 1.0, named)
    earlier = lax.broadcasted_iota(jnp.int32, (tok_dev, tok_dev), 0) < lax.broadcasted_iota(
        jnp.int32, (tok_dev, tok_dev), 1
    )
    rank = mul(named.astype(jnp.bfloat16), earlier.astype(jnp.bfloat16))
    rank = jnp.where(named > 0.0, rank, -1.0)
    out_ref[:, 2 * width :] = jnp.concatenate([weight, rank], axis=0).astype(jnp.bfloat16)


def pack(tokens, grad_out, routes, combine):
    tok_dev, width = tokens.shape
    return pl.pallas_call(
        pack_kernel,
        out_shape=jax.ShapeDtypeStruct((tok_dev, 2 * width + tok_dev), jnp.bfloat16),
        compiler_params=pltpu.CompilerParams(vmem_limit_bytes=VMEM_BYTES),
        cost_estimate=pl.CostEstimate(flops=10**7, bytes_accessed=2 * 10**6, transcendentals=0),
    )(tokens, grad_out, routes.T, combine.T)


def group_kernel(first, last, own, depth, blocks, *refs):
    refs = list(refs)

    def take(count):
        return [refs.pop(0) for _ in range(count)]

    block_hbm = take(blocks)
    weight_hbm = take(3)
    acc_hbm = [] if first else take(3)
    out_hbm = take(3)
    piece_hbm = take(2) if own else []
    block_buf, x_rows, d_rows, hid, both, info = take(6)
    weight_buf = gate_ref, up_ref, down_ref = take(3)
    acc_buf = take(3)
    out_buf = take(3) if last else acc_buf
    if own:
        back, places, *piece_buf = take(4)
    block_sem, weight_sem, acc_sem, out_sem, piece_sem = take(5)
    held, rows, width = x_rows.shape
    tok_dev = block_buf.shape[1]
    half = tok_dev // 2
    units = hid.shape[1]
    shard = lax.axis_index("dp")
    base = lax.axis_index("expert") * held
    x_cut = acc_buf[0].shape[1]
    h_cut = acc_buf[2].shape[1]

    def weight_in(e, m):
        return pltpu.make_async_copy(weight_hbm[m].at[e], weight_buf[m].at[e], weight_sem.at[m, e])

    def acc_in(e, m):
        return pltpu.make_async_copy(acc_hbm[m].at[e], acc_buf[m].at[e], acc_sem.at[m, e])

    def grad_out(e, m):
        return pltpu.make_async_copy(out_buf[m].at[e], out_hbm[m].at[e], out_sem.at[m, e])

    for b in range(blocks):
        pltpu.make_async_copy(block_hbm[b], block_buf.at[b], block_sem.at[b]).start()

    slot = lax.broadcasted_iota(jnp.int32, (depth, tok_dev), 0).astype(jnp.float32)

    def select(b, _):
        pltpu.make_async_copy(block_hbm[0], block_buf.at[b], block_sem.at[b]).wait()

        @pl.when(b == 1)
        def _():
            for m in range(3):
                weight_in(0, m).start()

        info[...] = block_buf[b, :, 2 * width :].astype(jnp.float32)
        picks, scaled = [], []
        for i in range(held):
            weight = info[pl.ds(base + i, 1), :]
            rank = info[pl.ds(half + base + i, 1), :]
            hit = slot == rank
            picks.append(jnp.where(hit, 1.0, 0.0))
            scaled.append(jnp.where(hit, weight, 0.0))
        pick = jnp.concatenate(picks, axis=0).astype(jnp.bfloat16)
        scale = jnp.concatenate(scaled, axis=0).astype(jnp.bfloat16)
        if own:

            @pl.when(b < own)
            def _():
                places[b] = pick

        got_x = mul(pick, block_buf[b, :, :width]).astype(jnp.bfloat16)
        got_d = mul(scale, block_buf[b, :, width : 2 * width]).astype(jnp.bfloat16)
        at = pl.ds(pl.multiple_of(b * depth, depth), depth)
        for i in range(held):
            x_rows[i, at, :] = got_x[i * depth : (i + 1) * depth]
            d_rows[i, at, :] = got_d[i * depth : (i + 1) * depth]
        return 0

    lax.fori_loop(0, blocks, select, 0)

    def expert(e, _):
        for m in range(3):
            weight_in(e, m).wait()
        for m in range(len(acc_hbm)):
            acc_in(e, m).start()

        @pl.when(e + 1 < held)
        def _():
            for m in range(3):
                weight_in(e + 1, m).start()

        rows_x = x_rows[e]
        d_out = d_rows[e]
        gate_pre = mul(rows_x, gate_ref[e])
        up_pre = mul(rows_x, up_ref[e])
        d_hidden = contract_last(d_out, down_ref[e])
        sig = 0.5 * jnp.tanh(0.5 * gate_pre) + 0.5
        act = gate_pre * sig
        hid[...] = (act * up_pre).astype(jnp.bfloat16)
        both[:, :units] = (d_hidden * up_pre * (sig + act * (1.0 - sig))).astype(jnp.bfloat16)
        both[:, units:] = (d_hidden * act).astype(jnp.bfloat16)
        x_part = x_rows[e, :, pl.ds(pl.multiple_of(shard * x_cut, LANES), x_cut)]
        h_part = hid[:, pl.ds(pl.multiple_of(shard * h_cut, LANES), h_cut)]
        grad_both = contract_first(x_part, both[...])
        grads = [grad_both[:, :units], grad_both[:, units:], contract_first(h_part, d_out)]
        for m in range(3):
            grad = grads[m]
            if not first:
                acc_in(e, m).wait()
                grad = acc_buf[m][e] + grad
            out_buf[m][e] = grad.astype(out_buf[m].dtype)
            grad_out(e, m).start()
        if own:
            kept = own * depth
            back[e] = (
                contract_last(both[:kept, :units], gate_ref[e])
                + contract_last(both[:kept, units:], up_ref[e])
            ).astype(jnp.bfloat16)
        return 0

    lax.fori_loop(0, held, expert, 0)

    if own:

        def collect(p, _):
            for odd in range(2):
                at = pl.ds(pl.multiple_of((2 * p + odd) * depth, depth), depth)
                rows_b = jnp.concatenate([back[i, at, :] for i in range(held)], axis=0)
                piece_buf[odd][p] = contract_first(places[2 * p + odd], rows_b).astype(
                    jnp.bfloat16
                )
            return 0

        lax.fori_loop(0, own // 2, collect, 0)
        pieces_out = [
            pltpu.make_async_copy(piece_buf[m], piece_hbm[m], piece_sem.at[m]) for m in range(2)
        ]
        for copy in pieces_out:
            copy.start()
        for copy in pieces_out:
            copy.wait()
    for e in range(held):
        for m in range(3):
            grad_out(e, m).wait()


def group(records, weights, accs, shards, depth, last=False, own=0):
    tok_dev, record = records[0].shape
    held, width, units = weights[0].shape
    blocks = len(records)
    rows = blocks * depth
    first = accs is None
    grad_shapes = [
        (held, width // shards, units),
        (held, width // shards, units),
        (held, units // shards, width),
    ]
    args = list(records) + list(weights) + ([] if first else list(accs))
    out_type = jnp.bfloat16 if last else jnp.float32
    out_shape = [jax.ShapeDtypeStruct(s, out_type) for s in grad_shapes]
    scratch = [
        pltpu.VMEM((blocks, tok_dev, record), jnp.bfloat16),
        pltpu.VMEM((held, rows, width), jnp.bfloat16),
        pltpu.VMEM((held, rows, width), jnp.bfloat16),
        pltpu.VMEM((rows, units), jnp.bfloat16),
        pltpu.VMEM((rows, 2 * units), jnp.bfloat16),
        pltpu.VMEM((tok_dev, tok_dev), jnp.float32),
    ]
    scratch += [pltpu.VMEM(w.shape, jnp.bfloat16) for w in weights]
    scratch += [pltpu.VMEM(s, jnp.float32) for s in grad_shapes]
    if last:
        scratch += [pltpu.VMEM(s, jnp.bfloat16) for s in grad_shapes]
    if own:
        piece = (own // 2, tok_dev, width)
        out_shape += [jax.ShapeDtypeStruct(piece, jnp.bfloat16)] * 2
        scratch += [
            pltpu.VMEM((held, own * depth, width), jnp.bfloat16),
            pltpu.VMEM((own, held * depth, tok_dev), jnp.bfloat16),
            pltpu.VMEM(piece, jnp.bfloat16),
            pltpu.VMEM(piece, jnp.bfloat16),
        ]
    scratch += [
        pltpu.SemaphoreType.DMA((blocks,)),
        pltpu.SemaphoreType.DMA((3, held)),
        pltpu.SemaphoreType.DMA((3, held)),
        pltpu.SemaphoreType.DMA((3, held)),
        pltpu.SemaphoreType.DMA((2,)),
    ]
    work = 2 * rows * held * width * units
    return pl.pallas_call(
        functools.partial(group_kernel, first, last, own, depth, blocks),
        in_specs=[pl.BlockSpec(memory_space=pl.ANY)] * len(args),
        out_specs=[pl.BlockSpec(memory_space=pl.ANY)] * len(out_shape),
        out_shape=out_shape,
        scratch_shapes=scratch,
        compiler_params=pltpu.CompilerParams(vmem_limit_bytes=VMEM_BYTES),
        cost_estimate=pl.CostEstimate(
            flops=work // 8,
            bytes_accessed=tok_dev * record * 2,
            transcendentals=rows * held * units,
        ),
    )(*args)


def swap(value, axis, bit):
    size = lax.axis_size(axis)
    return lax.ppermute(value, axis, [(i, i ^ bit) for i in range(size)])


def beside(value):
    return swap(value, "expert", 2)


def below(value):
    return swap(value, "expert", 4)


def pairs(*blocks):
    return [piece for block in blocks for piece in (block, swap(block, "expert", 1))]


def middle(value):
    return lax.ppermute(value, "dp", [(1, 2), (2, 1)])


def outward(value):
    return lax.ppermute(value, "dp", [(1, 0), (2, 3)])


def gathered_shards(tokens, grad_out, routes, combine, w_gate, w_up, w_down):
    shards = lax.axis_size("dp")
    tok_dev = tokens.shape[0]
    depth = depth_of(tok_dev, routes.shape[1], w_gate.shape[0] * lax.axis_size("expert"))
    run = functools.partial(
        group, weights=(w_gate, w_up, w_down), shards=shards, depth=depth
    )
    tie = lax.optimization_barrier
    inner = jnp.logical_and(lax.axis_index("dp") > 0, lax.axis_index("dp") < shards - 1)
    o0 = pack(tokens, grad_out, routes, combine)
    x0, y0, o1, near = beside(o0), below(o0), swap(o0, "dp", 1), middle(o0)
    group0 = pairs(o0)
    x0, y0, o1, near, group0 = tie((x0, y0, o1, near, group0))
    x1, d0, near_end, far = beside(o1), below(x0), outward(near), middle(o1)
    group0 += pairs(x0, y0, o1)
    y0, near, group0 = tie((y0, near, group0))
    *accs, even0, odd0 = run(group0, accs=None, own=6)
    x1, d0, near_end, near, far, even0, odd0, y0 = tie(
        (x1, d0, near_end, near, far, even0, odd0, y0)
    )
    o2 = jnp.where(inner, near, near_end)
    x2, y2, far_end, y1 = beside(o2), below(o2), outward(far), swap(y0, "dp", 1)
    crossed0 = swap(odd0, "expert", 1)
    group1 = pairs(d0, x1, o2)
    group1, crossed0, d0 = tie((group1, crossed0, d0))
    pair0 = (even0.astype(jnp.float32) + crossed0.astype(jnp.float32)).astype(jnp.bfloat16)
    *accs, even1, odd1 = run(group1, accs=accs, own=2)
    x2, y2, far_end, y1, far, d0, pair0, even1, odd1 = tie(
        (x2, y2, far_end, y1, far, d0, pair0, even1, odd1)
    )
    o3 = jnp.where(inner, far, far_end)
    x3, y3, d1, d2 = beside(o3), below(o3), swap(d0, "dp", 1), below(x2)
    crossed1 = swap(odd1, "expert", 1)
    group2 = pairs(x2, y2, o3, y1)
    group2, crossed1 = tie((group2, crossed1))
    pair1 = (even1.astype(jnp.float32) + crossed1.astype(jnp.float32)).astype(jnp.bfloat16)
    accs = run(group2, accs=accs)
    x3, y3, d1, d2, accs, pair1 = tie((x3, y3, d1, d2, accs, pair1))
    d3 = beside(y3)
    sent = [beside(pair0[1]), below(pair0[2]), swap(pair1[0], "expert", 6)]
    group3 = pairs(x3, y3, d1, d2)
    accs = run(group3, accs=accs)
    d3, accs, sent = tie((d3, accs, sent))
    total = pair0[0].astype(jnp.float32)
    for piece in sent:
        total = total + piece.astype(jnp.float32)
    accs = run(pairs(d3), accs=accs, last=True)
    return (total.astype(jnp.bfloat16), *accs)


def solution(mesh):
    shards, peers = mesh.shape["dp"], mesh.shape["expert"]

    def body(tokens, grad_out, routes, combine, w_gate, w_up, w_down):
        tok_dev, width = tokens.shape
        gathered = shards * peers * tok_dev * (2 * width + tok_dev) * 2
        fits = (
            peers == 8
            and shards == 4
            and peers * w_gate.shape[0] <= tok_dev // 2
            and tok_dev == LANES
            and gathered <= GATHER_BYTES
        )
        plan = gathered_shards if fits else routed_shards
        return plan(tokens, grad_out, routes, combine, w_gate, w_up, w_down)

    return jax.shard_map(
        body,
        mesh=mesh,
        in_specs=(
            P(("dp", "expert"), None),
            P(("dp", "expert"), None),
            P(("dp", "expert"), None),
            P(("dp", "expert"), None),
            P("expert", None, None),
            P("expert", None, None),
            P("expert", None, None),
        ),
        out_specs=(
            P(("dp", "expert"), None),
            P("expert", "dp", None),
            P("expert", "dp", None),
            P("expert", "dp", None),
        ),
        check_vma=False,
    )
```

```python
import functools
import jax
import jax.numpy as jnp
from jax import lax
from jax.experimental import pallas as pl
from jax.experimental.pallas import tpu as pltpu
from jax.sharding import PartitionSpec as P

LANES = 128
VMEM_BYTES = 26 * 1024 * 1024
GATHER_BYTES = 48 * 1024 * 1024


def slot_ranks(route_block, expert_total):
    flat_ids = route_block.reshape(-1)
    marks = (flat_ids[:, None] == jnp.arange(expert_total, dtype=jnp.int32)[None, :]).astype(
        jnp.int32
    )
    return jnp.sum((jnp.cumsum(marks, axis=0) - 1) * marks, axis=1)


def build_slots(route_block, expert_total, slot_depth):
    flat_ids = route_block.reshape(-1)
    pair_total = flat_ids.shape[0]
    slot_rank = slot_ranks(route_block, expert_total)
    slots = jnp.full((expert_total, slot_depth), pair_total, dtype=jnp.int32)
    slots = slots.at[flat_ids, slot_rank].set(jnp.arange(pair_total, dtype=jnp.int32))
    return (slots, slot_rank)


def contract_last(left, right):
    return lax.dot_general(
        left, right, (((1,), (1,)), ((), ())), preferred_element_type=jnp.float32
    )


def contract_first(left, right):
    return lax.dot_general(
        left, right, (((0,), (0,)), ((), ())), preferred_element_type=jnp.float32
    )


def mul(left, right):
    return jnp.dot(left, right, preferred_element_type=jnp.float32)


def depth_of(tok_dev, top_count, expert_total):
    return 8 * ((tok_dev * top_count * 6 // (5 * expert_total) + 7) // 8)


def expert_backward(rows_x, rows_dy, rows_c, gate_w, up_w, down_w):
    gate_pre = mul(rows_x, gate_w)
    up_pre = mul(rows_x, up_w)
    sigmoid_gate = jax.nn.sigmoid(gate_pre)
    hidden = (gate_pre * sigmoid_gate * up_pre).astype(jnp.bfloat16)
    d_out = (rows_c[:, None] * rows_dy.astype(jnp.float32)).astype(jnp.bfloat16)
    d_hidden = contract_last(d_out, down_w)
    d_gate = (d_hidden * up_pre * sigmoid_gate * (1.0 + gate_pre * (1.0 - sigmoid_gate))).astype(
        jnp.bfloat16
    )
    d_up = (d_hidden * gate_pre * sigmoid_gate).astype(jnp.bfloat16)
    d_rows = (contract_last(d_gate, gate_w) + contract_last(d_up, up_w)).astype(jnp.bfloat16)
    return (hidden, d_out, d_gate, d_up, d_rows)


def routed_shards(tokens, grad_out, routes, combine, w_gate, w_up, w_down):
    tok_dev, model_width = tokens.shape
    top_count = routes.shape[1]
    peer_count = lax.axis_size("expert")
    held_experts = w_gate.shape[0]
    hidden_units = w_gate.shape[2]
    expert_total = peer_count * held_experts
    slot_depth = depth_of(tok_dev, top_count, expert_total)
    pair_total = tok_dev * top_count
    slots, slot_rank = build_slots(routes, expert_total, slot_depth)
    filled = slots < pair_total
    token_index = jnp.where(filled, slots // top_count, tok_dev)
    pad_row = jnp.zeros((1, model_width), jnp.bfloat16)
    send_x = jnp.concatenate([tokens, pad_row])[token_index].reshape(
        peer_count, held_experts, slot_depth, model_width
    )
    send_dy = jnp.concatenate([grad_out, pad_row])[token_index].reshape(
        peer_count, held_experts, slot_depth, model_width
    )
    weight_ext = jnp.concatenate([combine.reshape(-1), jnp.zeros((1,), jnp.bfloat16)])
    send_c = weight_ext[slots].reshape(peer_count, held_experts, slot_depth)
    recv_x, recv_dy, recv_c = (
        lax.all_to_all(send_x, "expert", split_axis=0, concat_axis=0, tiled=True),
        lax.all_to_all(send_dy, "expert", split_axis=0, concat_axis=0, tiled=True),
        lax.all_to_all(send_c, "expert", split_axis=0, concat_axis=0, tiled=True),
    )
    gate_parts = []
    up_parts = []
    down_parts = []
    row_list = []
    for which in range(held_experts):
        rows_x = recv_x[:, which].reshape(-1, model_width)
        rows_dy = recv_dy[:, which].reshape(-1, model_width)
        rows_c = recv_c[:, which].reshape(-1).astype(jnp.float32)
        hidden, d_out, d_gate, d_up, d_rows = expert_backward(
            rows_x, rows_dy, rows_c, w_gate[which], w_up[which], w_down[which]
        )
        d_both = jnp.concatenate([d_gate, d_up], axis=1)
        row_list.append(d_rows.reshape(peer_count, slot_depth, model_width))
        summed = lax.psum_scatter(
            contract_first(rows_x, d_both).astype(jnp.bfloat16),
            "dp",
            scatter_dimension=0,
            tiled=True,
        ).astype(jnp.float32)
        gate_parts.append(summed[:, :hidden_units].astype(jnp.bfloat16))
        up_parts.append(summed[:, hidden_units:].astype(jnp.bfloat16))
        down_parts.append(
            lax.psum_scatter(
                contract_first(hidden, d_out).astype(jnp.bfloat16),
                "dp",
                scatter_dimension=0,
                tiled=True,
            )
        )
    grad_gate = jnp.stack(gate_parts)
    grad_up = jnp.stack(up_parts)
    grad_down = jnp.stack(down_parts)
    stacked = jnp.stack(row_list, axis=1)
    returned = lax.all_to_all(stacked, "expert", split_axis=0, concat_axis=0, tiled=True)
    flat_back = returned.reshape(expert_total * slot_depth, model_width)
    row_of_pair = routes.reshape(-1) * slot_depth + slot_rank
    per_pair = flat_back[row_of_pair].astype(jnp.float32).reshape(tok_dev, top_count, model_width)
    grad_tokens = jnp.sum(per_pair, axis=1).astype(jnp.bfloat16)
    return (grad_tokens, grad_gate, grad_up, grad_down)


def pack_kernel(tok_ref, dy_ref, routes_ref, combine_ref, out_ref):
    tok_dev, width = tok_ref.shape
    half = tok_dev // 2
    out_ref[:, :width] = tok_ref[...]
    out_ref[:, width : 2 * width] = dy_ref[...]
    ids = lax.broadcasted_iota(jnp.int32, (half, tok_dev), 0)
    weight = jnp.zeros((half, tok_dev), jnp.float32)
    named = jnp.zeros((half, tok_dev), jnp.float32)
    for k in range(routes_ref.shape[0]):
        hit = routes_ref[k : k + 1, :] == ids
        weight = jnp.where(hit, combine_ref[k : k + 1, :].astype(jnp.float32), weight)
        named = jnp.where(hit, 1.0, named)
    earlier = lax.broadcasted_iota(jnp.int32, (tok_dev, tok_dev), 0) < lax.broadcasted_iota(
        jnp.int32, (tok_dev, tok_dev), 1
    )
    rank = mul(named.astype(jnp.bfloat16), earlier.astype(jnp.bfloat16))
    rank = jnp.where(named > 0.0, rank, -1.0)
    out_ref[:, 2 * width :] = jnp.concatenate([weight, rank], axis=0).astype(jnp.bfloat16)


def pack(tokens, grad_out, routes, combine):
    tok_dev, width = tokens.shape
    return pl.pallas_call(
        pack_kernel,
        out_shape=jax.ShapeDtypeStruct((tok_dev, 2 * width + tok_dev), jnp.bfloat16),
        compiler_params=pltpu.CompilerParams(vmem_limit_bytes=VMEM_BYTES),
        cost_estimate=pl.CostEstimate(flops=10**7, bytes_accessed=2 * 10**6, transcendentals=0),
    )(tokens, grad_out, routes.T, combine.T)


def group_kernel(first, last, own, depth, blocks, *refs):
    refs = list(refs)

    def take(count):
        return [refs.pop(0) for _ in range(count)]

    block_hbm = take(blocks)
    gate_ref, up_ref, down_ref = take(3)
    acc_refs = [] if first else take(3)
    out_refs = take(3)
    piece_hbm = take(2) if own else []
    block_buf, x_rows, d_rows, hid, both, info = take(6)
    final_buf = take(3) if last else []
    if own:
        back, places, *piece_buf = take(4)
    block_sem, out_sem, piece_sem = take(3)
    held, rows, width = x_rows.shape
    tok_dev = block_buf.shape[1]
    half = tok_dev // 2
    units = hid.shape[1]
    shard = lax.axis_index("dp")
    base = lax.axis_index("expert") * held
    x_cut = out_refs[0].shape[1]
    h_cut = out_refs[2].shape[1]

    def grad_out(e, m):
        return pltpu.make_async_copy(final_buf[m].at[e], out_refs[m].at[e], out_sem.at[m, e])

    for b in range(blocks):
        pltpu.make_async_copy(block_hbm[b], block_buf.at[b], block_sem.at[b]).start()

    slot = lax.broadcasted_iota(jnp.int32, (depth, tok_dev), 0).astype(jnp.float32)

    def select(b, _):
        pltpu.make_async_copy(block_hbm[0], block_buf.at[b], block_sem.at[b]).wait()
        info[...] = block_buf[b, :, 2 * width :].astype(jnp.float32)
        picks, scaled = [], []
        for i in range(held):
            weight = info[pl.ds(base + i, 1), :]
            rank = info[pl.ds(half + base + i, 1), :]
            hit = slot == rank
            picks.append(jnp.where(hit, 1.0, 0.0))
            scaled.append(jnp.where(hit, weight, 0.0))
        pick = jnp.concatenate(picks, axis=0).astype(jnp.bfloat16)
        scale = jnp.concatenate(scaled, axis=0).astype(jnp.bfloat16)
        if own:

            @pl.when(b < own)
            def _():
                places[b] = pick

        got_x = mul(pick, block_buf[b, :, :width]).astype(jnp.bfloat16)
        got_d = mul(scale, block_buf[b, :, width : 2 * width]).astype(jnp.bfloat16)
        at = pl.ds(pl.multiple_of(b * depth, depth), depth)
        for i in range(held):
            x_rows[i, at, :] = got_x[i * depth : (i + 1) * depth]
            d_rows[i, at, :] = got_d[i * depth : (i + 1) * depth]
        return 0

    lax.fori_loop(0, blocks, select, 0)

    def expert(e, _):
        rows_x = x_rows[e]
        d_out = d_rows[e]
        gate_pre = mul(rows_x, gate_ref[e])
        up_pre = mul(rows_x, up_ref[e])
        d_hidden = contract_last(d_out, down_ref[e])
        sig = 0.5 * jnp.tanh(0.5 * gate_pre) + 0.5
        act = gate_pre * sig
        hid[...] = (act * up_pre).astype(jnp.bfloat16)
        both[:, :units] = (d_hidden * up_pre * (sig + act * (1.0 - sig))).astype(jnp.bfloat16)
        both[:, units:] = (d_hidden * act).astype(jnp.bfloat16)
        x_part = x_rows[e, :, pl.ds(pl.multiple_of(shard * x_cut, LANES), x_cut)]
        h_part = hid[:, pl.ds(pl.multiple_of(shard * h_cut, LANES), h_cut)]
        grad_both = contract_first(x_part, both[...])
        grads = [grad_both[:, :units], grad_both[:, units:], contract_first(h_part, d_out)]
        for m in range(3):
            grad = grads[m] if first else acc_refs[m][e] + grads[m]
            if last:
                final_buf[m][e] = grad.astype(jnp.bfloat16)
                grad_out(e, m).start()
            else:
                out_refs[m][e] = grad
        if own:
            kept = own * depth
            back[e] = (
                contract_last(both[:kept, :units], gate_ref[e])
                + contract_last(both[:kept, units:], up_ref[e])
            ).astype(jnp.bfloat16)
        return 0

    lax.fori_loop(0, held, expert, 0)

    if own:

        def collect(p, _):
            for odd in range(2):
                at = pl.ds(pl.multiple_of((2 * p + odd) * depth, depth), depth)
                rows_b = jnp.concatenate([back[i, at, :] for i in range(held)], axis=0)
                piece_buf[odd][p] = contract_first(places[2 * p + odd], rows_b).astype(
                    jnp.bfloat16
                )
            return 0

        lax.fori_loop(0, own // 2, collect, 0)
        pieces_out = [
            pltpu.make_async_copy(piece_buf[m], piece_hbm[m], piece_sem.at[m]) for m in range(2)
        ]
        for copy in pieces_out:
            copy.start()
        for copy in pieces_out:
            copy.wait()
    if last:
        for e in range(held):
            for m in range(3):
                grad_out(e, m).wait()


def group(records, weights, accs, shards, depth, last=False, own=0):
    tok_dev, record = records[0].shape
    held, width, units = weights[0].shape
    blocks = len(records)
    rows = blocks * depth
    first = accs is None
    grad_shapes = [
        (held, width // shards, units),
        (held, width // shards, units),
        (held, units // shards, width),
    ]
    args = list(records) + list(weights) + ([] if first else list(accs))
    out_type = jnp.bfloat16 if last else jnp.float32
    holder = jax.ShapeDtypeStruct if last else pltpu.VMEM
    out_shape = [holder(s, out_type) for s in grad_shapes]
    scratch = [
        pltpu.VMEM((blocks, tok_dev, record), jnp.bfloat16),
        pltpu.VMEM((held, rows, width), jnp.bfloat16),
        pltpu.VMEM((held, rows, width), jnp.bfloat16),
        pltpu.VMEM((rows, units), jnp.bfloat16),
        pltpu.VMEM((rows, 2 * units), jnp.bfloat16),
        pltpu.VMEM((tok_dev, tok_dev), jnp.float32),
    ]
    if last:
        scratch += [pltpu.VMEM(s, jnp.bfloat16) for s in grad_shapes]
    if own:
        piece = (own // 2, tok_dev, width)
        out_shape += [jax.ShapeDtypeStruct(piece, jnp.bfloat16)] * 2
        scratch += [
            pltpu.VMEM((held, own * depth, width), jnp.bfloat16),
            pltpu.VMEM((own, held * depth, tok_dev), jnp.bfloat16),
            pltpu.VMEM(piece, jnp.bfloat16),
            pltpu.VMEM(piece, jnp.bfloat16),
        ]
    scratch += [
        pltpu.SemaphoreType.DMA((blocks,)),
        pltpu.SemaphoreType.DMA((3, held)),
        pltpu.SemaphoreType.DMA((2,)),
    ]
    outside = pl.BlockSpec(memory_space=pltpu.HBM)
    inside = pl.BlockSpec(memory_space=pltpu.VMEM)
    work = 2 * rows * held * width * units
    return pl.pallas_call(
        functools.partial(group_kernel, first, last, own, depth, blocks),
        in_specs=[outside] * blocks + [inside] * (len(args) - blocks),
        out_specs=[outside if last else inside] * 3 + [outside] * (len(out_shape) - 3),
        input_output_aliases={} if first or last else {blocks + 3 + m: m for m in range(3)},
        out_shape=out_shape,
        scratch_shapes=scratch,
        compiler_params=pltpu.CompilerParams(vmem_limit_bytes=VMEM_BYTES),
        cost_estimate=pl.CostEstimate(
            flops=work // 8,
            bytes_accessed=tok_dev * record * 2,
            transcendentals=rows * held * units,
        ),
    )(*args)


def hold_kernel(*refs):
    sem = refs[-1]
    count = len(refs) // 2
    copies = [
        pltpu.make_async_copy(refs[m], refs[count + m], sem.at[m]) for m in range(count)
    ]
    for copy in copies:
        copy.start()
    for copy in copies:
        copy.wait()


def hold(*arrays):
    return pl.pallas_call(
        hold_kernel,
        in_specs=[pl.BlockSpec(memory_space=pl.ANY)] * len(arrays),
        out_specs=[pl.BlockSpec(memory_space=pltpu.VMEM)] * len(arrays),
        out_shape=[pltpu.VMEM(a.shape, a.dtype) for a in arrays],
        scratch_shapes=[pltpu.SemaphoreType.DMA((len(arrays),))],
        compiler_params=pltpu.CompilerParams(vmem_limit_bytes=2 * VMEM_BYTES),
        cost_estimate=pl.CostEstimate(flops=0, bytes_accessed=2 * 10**6, transcendentals=0),
    )(*arrays)


def swap(value, axis, bit):
    size = lax.axis_size(axis)
    return lax.ppermute(value, axis, [(i, i ^ bit) for i in range(size)])


def beside(value):
    return swap(value, "expert", 2)


def below(value):
    return swap(value, "expert", 4)


def pairs(*blocks):
    return [piece for block in blocks for piece in (block, swap(block, "expert", 1))]


def middle(value):
    return lax.ppermute(value, "dp", [(1, 2), (2, 1)])


def outward(value):
    return lax.ppermute(value, "dp", [(1, 0), (2, 3)])


def gathered_shards(tokens, grad_out, routes, combine, w_gate, w_up, w_down):
    shards = lax.axis_size("dp")
    tok_dev = tokens.shape[0]
    depth = depth_of(tok_dev, routes.shape[1], w_gate.shape[0] * lax.axis_size("expert"))
    tie = lax.optimization_barrier
    inner = jnp.logical_and(lax.axis_index("dp") > 0, lax.axis_index("dp") < shards - 1)
    o0 = pack(tokens, grad_out, routes, combine)
    x0, y0, o1, near = beside(o0), below(o0), swap(o0, "dp", 1), middle(o0)
    group0 = pairs(o0)
    weights = hold(*tie((w_gate, w_up, w_down, o0))[:3])
    x0, y0, o1, near, group0, weights = tie((x0, y0, o1, near, group0, weights))
    run = functools.partial(group, weights=weights, shards=shards, depth=depth)
    x1, d0, near_end, far = beside(o1), below(x0), outward(near), middle(o1)
    group0 += pairs(x0, y0, o1)
    y0, near, group0 = tie((y0, near, group0))
    *accs, even0, odd0 = run(group0, accs=None, own=6)
    x1, d0, near_end, near, far, even0, odd0, y0 = tie(
        (x1, d0, near_end, near, far, even0, odd0, y0)
    )
    o2 = jnp.where(inner, near, near_end)
    x2, y2, far_end = beside(o2), below(o2), outward(far)
    crossed0 = swap(odd0, "expert", 1)
    group1 = pairs(d0, x1, o2)
    group1, crossed0, d0 = tie((group1, crossed0, d0))
    pair0 = (even0.astype(jnp.float32) + crossed0.astype(jnp.float32)).astype(jnp.bfloat16)
    *accs, even1, odd1 = run(group1, accs=accs, own=2)
    x2, y2, far_end, y0, far, d0, pair0, even1, odd1 = tie(
        (x2, y2, far_end, y0, far, d0, pair0, even1, odd1)
    )
    o3 = jnp.where(inner, far, far_end)
    x3, y3, y1, d2 = beside(o3), below(o3), swap(y0, "dp", 1), below(x2)
    crossed1 = swap(odd1, "expert", 1)
    group2 = pairs(x2, y2, o3)
    group2, crossed1 = tie((group2, crossed1))
    pair1 = (even1.astype(jnp.float32) + crossed1.astype(jnp.float32)).astype(jnp.bfloat16)
    accs = run(group2, accs=accs)
    x3, y3, y1, d2, accs, pair1, d0 = tie((x3, y3, y1, d2, accs, pair1, d0))
    d3, d1 = beside(y3), swap(d0, "dp", 1)
    sent = [beside(pair0[1]), below(pair0[2]), swap(pair1[0], "expert", 6)]
    group3 = pairs(x3, y3, y1, d2)
    accs = run(group3, accs=accs)
    d3, d1, accs, sent = tie((d3, d1, accs, sent))
    total = pair0[0].astype(jnp.float32)
    for piece in sent:
        total = total + piece.astype(jnp.float32)
    accs = run(pairs(d1, d3), accs=accs, last=True)
    return (total.astype(jnp.bfloat16), *accs)


def solution(mesh):
    shards, peers = mesh.shape["dp"], mesh.shape["expert"]

    def body(tokens, grad_out, routes, combine, w_gate, w_up, w_down):
        tok_dev, width = tokens.shape
        gathered = shards * peers * tok_dev * (2 * width + tok_dev) * 2
        fits = (
            peers == 8
            and shards == 4
            and peers * w_gate.shape[0] <= tok_dev // 2
            and tok_dev == LANES
            and gathered <= GATHER_BYTES
        )
        plan = gathered_shards if fits else routed_shards
        return plan(tokens, grad_out, routes, combine, w_gate, w_up, w_down)

    return jax.shard_map(
        body,
        mesh=mesh,
        in_specs=(
            P(("dp", "expert"), None),
            P(("dp", "expert"), None),
            P(("dp", "expert"), None),
            P(("dp", "expert"), None),
            P("expert", None, None),
            P("expert", None, None),
            P("expert", None, None),
        ),
        out_specs=(
            P(("dp", "expert"), None),
            P("expert", "dp", None),
            P("expert", "dp", None),
            P("expert", "dp", None),
        ),
        check_vma=False,
    )
```

```python
import functools
import jax
import jax.numpy as jnp
from jax import lax
from jax.experimental import pallas as pl
from jax.experimental.pallas import tpu as pltpu
from jax.sharding import PartitionSpec as P

LANES = 128
VMEM_BYTES = 26 * 1024 * 1024
GATHER_BYTES = 48 * 1024 * 1024


def slot_ranks(route_block, expert_total):
    flat_ids = route_block.reshape(-1)
    marks = (flat_ids[:, None] == jnp.arange(expert_total, dtype=jnp.int32)[None, :]).astype(
        jnp.int32
    )
    return jnp.sum((jnp.cumsum(marks, axis=0) - 1) * marks, axis=1)


def build_slots(route_block, expert_total, slot_depth):
    flat_ids = route_block.reshape(-1)
    pair_total = flat_ids.shape[0]
    slot_rank = slot_ranks(route_block, expert_total)
    slots = jnp.full((expert_total, slot_depth), pair_total, dtype=jnp.int32)
    slots = slots.at[flat_ids, slot_rank].set(jnp.arange(pair_total, dtype=jnp.int32))
    return (slots, slot_rank)


def contract_last(left, right):
    return lax.dot_general(
        left, right, (((1,), (1,)), ((), ())), preferred_element_type=jnp.float32
    )


def contract_first(left, right):
    return lax.dot_general(
        left, right, (((0,), (0,)), ((), ())), preferred_element_type=jnp.float32
    )


def mul(left, right):
    return jnp.dot(left, right, preferred_element_type=jnp.float32)


def depth_of(tok_dev, top_count, expert_total):
    return 8 * ((tok_dev * top_count * 6 // (5 * expert_total) + 7) // 8)


def expert_backward(rows_x, rows_dy, rows_c, gate_w, up_w, down_w):
    gate_pre = mul(rows_x, gate_w)
    up_pre = mul(rows_x, up_w)
    sigmoid_gate = jax.nn.sigmoid(gate_pre)
    hidden = (gate_pre * sigmoid_gate * up_pre).astype(jnp.bfloat16)
    d_out = (rows_c[:, None] * rows_dy.astype(jnp.float32)).astype(jnp.bfloat16)
    d_hidden = contract_last(d_out, down_w)
    d_gate = (d_hidden * up_pre * sigmoid_gate * (1.0 + gate_pre * (1.0 - sigmoid_gate))).astype(
        jnp.bfloat16
    )
    d_up = (d_hidden * gate_pre * sigmoid_gate).astype(jnp.bfloat16)
    d_rows = (contract_last(d_gate, gate_w) + contract_last(d_up, up_w)).astype(jnp.bfloat16)
    return (hidden, d_out, d_gate, d_up, d_rows)


def routed_shards(tokens, grad_out, routes, combine, w_gate, w_up, w_down):
    tok_dev, model_width = tokens.shape
    top_count = routes.shape[1]
    peer_count = lax.axis_size("expert")
    held_experts = w_gate.shape[0]
    hidden_units = w_gate.shape[2]
    expert_total = peer_count * held_experts
    slot_depth = depth_of(tok_dev, top_count, expert_total)
    pair_total = tok_dev * top_count
    slots, slot_rank = build_slots(routes, expert_total, slot_depth)
    filled = slots < pair_total
    token_index = jnp.where(filled, slots // top_count, tok_dev)
    pad_row = jnp.zeros((1, model_width), jnp.bfloat16)
    send_x = jnp.concatenate([tokens, pad_row])[token_index].reshape(
        peer_count, held_experts, slot_depth, model_width
    )
    send_dy = jnp.concatenate([grad_out, pad_row])[token_index].reshape(
        peer_count, held_experts, slot_depth, model_width
    )
    weight_ext = jnp.concatenate([combine.reshape(-1), jnp.zeros((1,), jnp.bfloat16)])
    send_c = weight_ext[slots].reshape(peer_count, held_experts, slot_depth)
    recv_x, recv_dy, recv_c = (
        lax.all_to_all(send_x, "expert", split_axis=0, concat_axis=0, tiled=True),
        lax.all_to_all(send_dy, "expert", split_axis=0, concat_axis=0, tiled=True),
        lax.all_to_all(send_c, "expert", split_axis=0, concat_axis=0, tiled=True),
    )
    gate_parts = []
    up_parts = []
    down_parts = []
    row_list = []
    for which in range(held_experts):
        rows_x = recv_x[:, which].reshape(-1, model_width)
        rows_dy = recv_dy[:, which].reshape(-1, model_width)
        rows_c = recv_c[:, which].reshape(-1).astype(jnp.float32)
        hidden, d_out, d_gate, d_up, d_rows = expert_backward(
            rows_x, rows_dy, rows_c, w_gate[which], w_up[which], w_down[which]
        )
        d_both = jnp.concatenate([d_gate, d_up], axis=1)
        row_list.append(d_rows.reshape(peer_count, slot_depth, model_width))
        summed = lax.psum_scatter(
            contract_first(rows_x, d_both).astype(jnp.bfloat16),
            "dp",
            scatter_dimension=0,
            tiled=True,
        ).astype(jnp.float32)
        gate_parts.append(summed[:, :hidden_units].astype(jnp.bfloat16))
        up_parts.append(summed[:, hidden_units:].astype(jnp.bfloat16))
        down_parts.append(
            lax.psum_scatter(
                contract_first(hidden, d_out).astype(jnp.bfloat16),
                "dp",
                scatter_dimension=0,
                tiled=True,
            )
        )
    grad_gate = jnp.stack(gate_parts)
    grad_up = jnp.stack(up_parts)
    grad_down = jnp.stack(down_parts)
    stacked = jnp.stack(row_list, axis=1)
    returned = lax.all_to_all(stacked, "expert", split_axis=0, concat_axis=0, tiled=True)
    flat_back = returned.reshape(expert_total * slot_depth, model_width)
    row_of_pair = routes.reshape(-1) * slot_depth + slot_rank
    per_pair = flat_back[row_of_pair].astype(jnp.float32).reshape(tok_dev, top_count, model_width)
    grad_tokens = jnp.sum(per_pair, axis=1).astype(jnp.bfloat16)
    return (grad_tokens, grad_gate, grad_up, grad_down)


def pack_kernel(tok_ref, dy_ref, routes_ref, combine_ref, out_ref):
    tok_dev, width = tok_ref.shape
    half = tok_dev // 2
    out_ref[:, :width] = tok_ref[...]
    out_ref[:, width : 2 * width] = dy_ref[...]
    ids = lax.broadcasted_iota(jnp.int32, (half, tok_dev), 0)
    weight = jnp.zeros((half, tok_dev), jnp.float32)
    named = jnp.zeros((half, tok_dev), jnp.float32)
    for k in range(routes_ref.shape[0]):
        hit = routes_ref[k : k + 1, :] == ids
        weight = jnp.where(hit, combine_ref[k : k + 1, :].astype(jnp.float32), weight)
        named = jnp.where(hit, 1.0, named)
    earlier = lax.broadcasted_iota(jnp.int32, (tok_dev, tok_dev), 0) < lax.broadcasted_iota(
        jnp.int32, (tok_dev, tok_dev), 1
    )
    rank = mul(named.astype(jnp.bfloat16), earlier.astype(jnp.bfloat16))
    rank = jnp.where(named > 0.0, rank, -1.0)
    out_ref[:, 2 * width :] = jnp.concatenate([weight, rank], axis=0).astype(jnp.bfloat16)


def pack(tokens, grad_out, routes, combine):
    tok_dev, width = tokens.shape
    return pl.pallas_call(
        pack_kernel,
        out_shape=jax.ShapeDtypeStruct((tok_dev, 2 * width + tok_dev), jnp.bfloat16),
        compiler_params=pltpu.CompilerParams(vmem_limit_bytes=2 * VMEM_BYTES),
        cost_estimate=pl.CostEstimate(flops=10**7, bytes_accessed=2 * 10**6, transcendentals=0),
    )(tokens, grad_out, routes.T, combine.T)


def group_kernel(first, last, own, depth, blocks, *refs):
    refs = list(refs)

    def take(count):
        return [refs.pop(0) for _ in range(count)]

    block_hbm = take(blocks)
    gate_ref, up_ref, down_ref = take(3)
    acc_refs = [] if first else take(3)
    out_refs = take(3)
    piece_hbm = take(2) if own else []
    block_buf, x_rows, d_rows, hid, both, info = take(6)
    final_buf = take(3) if last else []
    if own:
        back, places, *piece_buf = take(4)
    block_sem, out_sem, piece_sem = take(3)
    held, rows, width = x_rows.shape
    tok_dev = block_buf.shape[1]
    half = tok_dev // 2
    units = hid.shape[1]
    shard = lax.axis_index("dp")
    base = lax.axis_index("expert") * held
    x_cut = out_refs[0].shape[1]
    h_cut = out_refs[2].shape[1]

    def grad_out(e, m):
        return pltpu.make_async_copy(final_buf[m].at[e], out_refs[m].at[e], out_sem.at[m, e])

    for b in range(blocks):
        pltpu.make_async_copy(block_hbm[b], block_buf.at[b], block_sem.at[b]).start()

    slot = lax.broadcasted_iota(jnp.int32, (depth, tok_dev), 0).astype(jnp.float32)

    def select(b, _):
        pltpu.make_async_copy(block_hbm[0], block_buf.at[b], block_sem.at[b]).wait()
        info[...] = block_buf[b, :, 2 * width :].astype(jnp.float32)
        picks, scaled = [], []
        for i in range(held):
            weight = info[pl.ds(base + i, 1), :]
            rank = info[pl.ds(half + base + i, 1), :]
            hit = slot == rank
            picks.append(jnp.where(hit, 1.0, 0.0))
            scaled.append(jnp.where(hit, weight, 0.0))
        pick = jnp.concatenate(picks, axis=0).astype(jnp.bfloat16)
        scale = jnp.concatenate(scaled, axis=0).astype(jnp.bfloat16)
        if own:

            @pl.when(b < own)
            def _():
                places[b] = pick

        got_x = mul(pick, block_buf[b, :, :width]).astype(jnp.bfloat16)
        got_d = mul(scale, block_buf[b, :, width : 2 * width]).astype(jnp.bfloat16)
        at = pl.ds(pl.multiple_of(b * depth, depth), depth)
        for i in range(held):
            x_rows[i, at, :] = got_x[i * depth : (i + 1) * depth]
            d_rows[i, at, :] = got_d[i * depth : (i + 1) * depth]
        return 0

    lax.fori_loop(0, blocks, select, 0)

    def expert(e, _):
        rows_x = x_rows[e]
        d_out = d_rows[e]
        gate_pre = mul(rows_x, gate_ref[e])
        up_pre = mul(rows_x, up_ref[e])
        d_hidden = contract_last(d_out, down_ref[e])
        sig = 0.5 * jnp.tanh(0.5 * gate_pre) + 0.5
        act = gate_pre * sig
        hid[...] = (act * up_pre).astype(jnp.bfloat16)
        both[:, :units] = (d_hidden * up_pre * (sig + act * (1.0 - sig))).astype(jnp.bfloat16)
        both[:, units:] = (d_hidden * act).astype(jnp.bfloat16)
        x_part = x_rows[e, :, pl.ds(pl.multiple_of(shard * x_cut, LANES), x_cut)]
        h_part = hid[:, pl.ds(pl.multiple_of(shard * h_cut, LANES), h_cut)]
        grad_both = contract_first(x_part, both[...])
        grads = [grad_both[:, :units], grad_both[:, units:], contract_first(h_part, d_out)]
        for m in range(3):
            grad = grads[m] if first else acc_refs[m][e] + grads[m]
            if last:
                final_buf[m][e] = grad.astype(jnp.bfloat16)
                grad_out(e, m).start()
            else:
                out_refs[m][e] = grad
        if own:
            kept = own * depth
            back[e] = (
                contract_last(both[:kept, :units], gate_ref[e])
                + contract_last(both[:kept, units:], up_ref[e])
            ).astype(jnp.bfloat16)
        return 0

    lax.fori_loop(0, held, expert, 0)

    if own:

        def collect(p, _):
            for odd in range(2):
                at = pl.ds(pl.multiple_of((2 * p + odd) * depth, depth), depth)
                rows_b = jnp.concatenate([back[i, at, :] for i in range(held)], axis=0)
                piece_buf[odd][p] = contract_first(places[2 * p + odd], rows_b).astype(
                    jnp.bfloat16
                )
            return 0

        lax.fori_loop(0, own // 2, collect, 0)
        pieces_out = [
            pltpu.make_async_copy(piece_buf[m], piece_hbm[m], piece_sem.at[m]) for m in range(2)
        ]
        for copy in pieces_out:
            copy.start()
        for copy in pieces_out:
            copy.wait()
    if last:
        for e in range(held):
            for m in range(3):
                grad_out(e, m).wait()


def group(records, weights, accs, shards, depth, last=False, own=0):
    tok_dev, record = records[0].shape
    held, width, units = weights[0].shape
    blocks = len(records)
    rows = blocks * depth
    first = accs is None
    grad_shapes = [
        (held, width // shards, units),
        (held, width // shards, units),
        (held, units // shards, width),
    ]
    args = list(records) + list(weights) + ([] if first else list(accs))
    out_type = jnp.bfloat16 if last else jnp.float32
    holder = jax.ShapeDtypeStruct if last else pltpu.VMEM
    out_shape = [holder(s, out_type) for s in grad_shapes]
    scratch = [
        pltpu.VMEM((blocks, tok_dev, record), jnp.bfloat16),
        pltpu.VMEM((held, rows, width), jnp.bfloat16),
        pltpu.VMEM((held, rows, width), jnp.bfloat16),
        pltpu.VMEM((rows, units), jnp.bfloat16),
        pltpu.VMEM((rows, 2 * units), jnp.bfloat16),
        pltpu.VMEM((tok_dev, tok_dev), jnp.float32),
    ]
    if last:
        scratch += [pltpu.VMEM(s, jnp.bfloat16) for s in grad_shapes]
    if own:
        piece = (own // 2, tok_dev, width)
        out_shape += [jax.ShapeDtypeStruct(piece, jnp.bfloat16)] * 2
        scratch += [
            pltpu.VMEM((held, own * depth, width), jnp.bfloat16),
            pltpu.VMEM((own, held * depth, tok_dev), jnp.bfloat16),
            pltpu.VMEM(piece, jnp.bfloat16),
            pltpu.VMEM(piece, jnp.bfloat16),
        ]
    scratch += [
        pltpu.SemaphoreType.DMA((blocks,)),
        pltpu.SemaphoreType.DMA((3, held)),
        pltpu.SemaphoreType.DMA((2,)),
    ]
    outside = pl.BlockSpec(memory_space=pltpu.HBM)
    inside = pl.BlockSpec(memory_space=pltpu.VMEM)
    work = 2 * rows * held * width * units
    return pl.pallas_call(
        functools.partial(group_kernel, first, last, own, depth, blocks),
        in_specs=[outside] * blocks + [inside] * (len(args) - blocks),
        out_specs=[outside if last else inside] * 3 + [outside] * (len(out_shape) - 3),
        input_output_aliases={} if first or last else {blocks + 3 + m: m for m in range(3)},
        out_shape=out_shape,
        scratch_shapes=scratch,
        compiler_params=pltpu.CompilerParams(vmem_limit_bytes=VMEM_BYTES),
        cost_estimate=pl.CostEstimate(
            flops=work // 8,
            bytes_accessed=tok_dev * record * 2,
            transcendentals=rows * held * units,
        ),
    )(*args)


def hold_kernel(*refs):
    sem = refs[-1]
    count = len(refs) // 2
    copies = [
        pltpu.make_async_copy(refs[m], refs[count + m], sem.at[m]) for m in range(count)
    ]
    for copy in copies:
        copy.start()
    for copy in copies:
        copy.wait()


def hold(*arrays):
    return pl.pallas_call(
        hold_kernel,
        in_specs=[pl.BlockSpec(memory_space=pl.ANY)] * len(arrays),
        out_specs=[pl.BlockSpec(memory_space=pltpu.VMEM)] * len(arrays),
        out_shape=[pltpu.VMEM(a.shape, a.dtype) for a in arrays],
        scratch_shapes=[pltpu.SemaphoreType.DMA((len(arrays),))],
        compiler_params=pltpu.CompilerParams(vmem_limit_bytes=2 * VMEM_BYTES),
        cost_estimate=pl.CostEstimate(flops=0, bytes_accessed=2 * 10**6, transcendentals=0),
    )(*arrays)


def choose_kernel(inner_ref, outer_ref, out_ref, sem):
    place = lax.axis_index("dp")
    inner = jnp.logical_and(place > 0, place < lax.axis_size("dp") - 1)

    @pl.when(inner)
    def _():
        copy = pltpu.make_async_copy(inner_ref, out_ref, sem)
        copy.start()
        copy.wait()

    @pl.when(jnp.logical_not(inner))
    def _():
        copy = pltpu.make_async_copy(outer_ref, out_ref, sem)
        copy.start()
        copy.wait()


def choose(inner, outer):
    return pl.pallas_call(
        choose_kernel,
        in_specs=[pl.BlockSpec(memory_space=pltpu.HBM)] * 2,
        out_specs=pl.BlockSpec(memory_space=pltpu.HBM),
        out_shape=pltpu.HBM(inner.shape, inner.dtype),
        scratch_shapes=[pltpu.SemaphoreType.DMA],
        compiler_params=pltpu.CompilerParams(vmem_limit_bytes=VMEM_BYTES),
        cost_estimate=pl.CostEstimate(flops=0, bytes_accessed=10**6, transcendentals=0),
    )(inner, outer)


def swap(value, axis, bit):
    size = lax.axis_size(axis)
    return lax.ppermute(value, axis, [(i, i ^ bit) for i in range(size)])


def beside(value):
    return swap(value, "expert", 2)


def below(value):
    return swap(value, "expert", 4)


def pairs(*blocks):
    return [piece for block in blocks for piece in (block, swap(block, "expert", 1))]


def middle(value):
    return lax.ppermute(value, "dp", [(1, 2), (2, 1)])


def outward(value):
    return lax.ppermute(value, "dp", [(1, 0), (2, 3)])


def gathered_shards(tokens, grad_out, routes, combine, w_gate, w_up, w_down):
    shards = lax.axis_size("dp")
    tok_dev = tokens.shape[0]
    depth = depth_of(tok_dev, routes.shape[1], w_gate.shape[0] * lax.axis_size("expert"))
    tie = lax.optimization_barrier
    o0 = pack(tokens, grad_out, routes, combine)
    x0, y0, o1, near = beside(o0), below(o0), swap(o0, "dp", 1), middle(o0)
    group0 = pairs(o0)
    weights = hold(*tie((w_gate, w_up, w_down, o0))[:3])
    x0, y0, o1, near, group0, weights = tie((x0, y0, o1, near, group0, weights))
    run = functools.partial(group, weights=weights, shards=shards, depth=depth)
    x1, d0, near_end, far = beside(o1), below(x0), outward(near), middle(o1)
    group0 += pairs(x0, y0, o1)
    y0, near, group0 = tie((y0, near, group0))
    *accs, even0, odd0 = run(group0, accs=None, own=6)
    x1, d0, near_end, near, far, even0, odd0, y0 = tie(
        (x1, d0, near_end, near, far, even0, odd0, y0)
    )
    o2 = choose(near, near_end)
    x2, y2, far_end = beside(o2), below(o2), outward(far)
    crossed0 = swap(odd0, "expert", 1)
    group1 = pairs(d0, x1, o2)
    group1, crossed0, d0 = tie((group1, crossed0, d0))
    pair0 = (even0.astype(jnp.float32) + crossed0.astype(jnp.float32)).astype(jnp.bfloat16)
    *accs, even1, odd1 = run(group1, accs=accs, own=2)
    x2, y2, far_end, y0, far, d0, pair0, even1, odd1 = tie(
        (x2, y2, far_end, y0, far, d0, pair0, even1, odd1)
    )
    o3 = choose(far, far_end)
    x3, y3, y1 = beside(o3), below(o3), swap(y0, "dp", 1)
    sent = [beside(pair0[1]), below(pair0[2])]
    crossed1 = swap(odd1, "expert", 1)
    group2 = pairs(x2, y2, o3)
    group2, crossed1 = tie((group2, crossed1))
    pair1 = (even1.astype(jnp.float32) + crossed1.astype(jnp.float32)).astype(jnp.bfloat16)
    accs = run(group2, accs=accs)
    x3, y3, y1, accs, pair1, d0, x2, sent = tie((x3, y3, y1, accs, pair1, d0, x2, sent))
    d3, d2, d1 = beside(y3), below(x2), swap(d0, "dp", 1)
    sent.append(swap(pair1[0], "expert", 6))
    accs = run(pairs(x3, y3, y1), accs=accs)
    d3, d2, d1, accs, sent = tie((d3, d2, d1, accs, sent))
    total = pair0[0].astype(jnp.float32)
    for piece in sent:
        total = total + piece.astype(jnp.float32)
    accs = run(pairs(d1, d2, d3), accs=accs, last=True)
    return (total.astype(jnp.bfloat16), *accs)


def solution(mesh):
    shards, peers = mesh.shape["dp"], mesh.shape["expert"]

    def body(tokens, grad_out, routes, combine, w_gate, w_up, w_down):
        tok_dev, width = tokens.shape
        gathered = shards * peers * tok_dev * (2 * width + tok_dev) * 2
        fits = (
            peers == 8
            and shards == 4
            and peers * w_gate.shape[0] <= tok_dev // 2
            and tok_dev == LANES
            and gathered <= GATHER_BYTES
        )
        plan = gathered_shards if fits else routed_shards
        return plan(tokens, grad_out, routes, combine, w_gate, w_up, w_down)

    return jax.shard_map(
        body,
        mesh=mesh,
        in_specs=(
            P(("dp", "expert"), None),
            P(("dp", "expert"), None),
            P(("dp", "expert"), None),
            P(("dp", "expert"), None),
            P("expert", None, None),
            P("expert", None, None),
            P("expert", None, None),
        ),
        out_specs=(
            P(("dp", "expert"), None),
            P("expert", "dp", None),
            P("expert", "dp", None),
            P("expert", "dp", None),
        ),
        check_vma=False,
    )
```

```python
import functools
import jax
import jax.numpy as jnp
from jax import lax
from jax.experimental import pallas as pl
from jax.experimental.pallas import tpu as pltpu
from jax.sharding import PartitionSpec as P

LANES = 128
VMEM_BYTES = 26 * 1024 * 1024
GATHER_BYTES = 48 * 1024 * 1024


def slot_ranks(route_block, expert_total):
    flat_ids = route_block.reshape(-1)
    marks = (flat_ids[:, None] == jnp.arange(expert_total, dtype=jnp.int32)[None, :]).astype(
        jnp.int32
    )
    return jnp.sum((jnp.cumsum(marks, axis=0) - 1) * marks, axis=1)


def build_slots(route_block, expert_total, slot_depth):
    flat_ids = route_block.reshape(-1)
    pair_total = flat_ids.shape[0]
    slot_rank = slot_ranks(route_block, expert_total)
    slots = jnp.full((expert_total, slot_depth), pair_total, dtype=jnp.int32)
    slots = slots.at[flat_ids, slot_rank].set(jnp.arange(pair_total, dtype=jnp.int32))
    return (slots, slot_rank)


def contract_last(left, right):
    return lax.dot_general(
        left, right, (((1,), (1,)), ((), ())), preferred_element_type=jnp.float32
    )


def contract_first(left, right):
    return lax.dot_general(
        left, right, (((0,), (0,)), ((), ())), preferred_element_type=jnp.float32
    )


def mul(left, right):
    return jnp.dot(left, right, preferred_element_type=jnp.float32)


def depth_of(tok_dev, top_count, expert_total):
    return 8 * ((tok_dev * top_count * 6 // (5 * expert_total) + 7) // 8)


def expert_backward(rows_x, rows_dy, rows_c, gate_w, up_w, down_w):
    gate_pre = mul(rows_x, gate_w)
    up_pre = mul(rows_x, up_w)
    sigmoid_gate = jax.nn.sigmoid(gate_pre)
    hidden = (gate_pre * sigmoid_gate * up_pre).astype(jnp.bfloat16)
    d_out = (rows_c[:, None] * rows_dy.astype(jnp.float32)).astype(jnp.bfloat16)
    d_hidden = contract_last(d_out, down_w)
    d_gate = (d_hidden * up_pre * sigmoid_gate * (1.0 + gate_pre * (1.0 - sigmoid_gate))).astype(
        jnp.bfloat16
    )
    d_up = (d_hidden * gate_pre * sigmoid_gate).astype(jnp.bfloat16)
    d_rows = (contract_last(d_gate, gate_w) + contract_last(d_up, up_w)).astype(jnp.bfloat16)
    return (hidden, d_out, d_gate, d_up, d_rows)


def routed_shards(tokens, grad_out, routes, combine, w_gate, w_up, w_down):
    tok_dev, model_width = tokens.shape
    top_count = routes.shape[1]
    peer_count = lax.axis_size("expert")
    held_experts = w_gate.shape[0]
    hidden_units = w_gate.shape[2]
    expert_total = peer_count * held_experts
    slot_depth = depth_of(tok_dev, top_count, expert_total)
    pair_total = tok_dev * top_count
    slots, slot_rank = build_slots(routes, expert_total, slot_depth)
    filled = slots < pair_total
    token_index = jnp.where(filled, slots // top_count, tok_dev)
    pad_row = jnp.zeros((1, model_width), jnp.bfloat16)
    send_x = jnp.concatenate([tokens, pad_row])[token_index].reshape(
        peer_count, held_experts, slot_depth, model_width
    )
    send_dy = jnp.concatenate([grad_out, pad_row])[token_index].reshape(
        peer_count, held_experts, slot_depth, model_width
    )
    weight_ext = jnp.concatenate([combine.reshape(-1), jnp.zeros((1,), jnp.bfloat16)])
    send_c = weight_ext[slots].reshape(peer_count, held_experts, slot_depth)
    recv_x, recv_dy, recv_c = (
        lax.all_to_all(send_x, "expert", split_axis=0, concat_axis=0, tiled=True),
        lax.all_to_all(send_dy, "expert", split_axis=0, concat_axis=0, tiled=True),
        lax.all_to_all(send_c, "expert", split_axis=0, concat_axis=0, tiled=True),
    )
    gate_parts = []
    up_parts = []
    down_parts = []
    row_list = []
    for which in range(held_experts):
        rows_x = recv_x[:, which].reshape(-1, model_width)
        rows_dy = recv_dy[:, which].reshape(-1, model_width)
        rows_c = recv_c[:, which].reshape(-1).astype(jnp.float32)
        hidden, d_out, d_gate, d_up, d_rows = expert_backward(
            rows_x, rows_dy, rows_c, w_gate[which], w_up[which], w_down[which]
        )
        d_both = jnp.concatenate([d_gate, d_up], axis=1)
        row_list.append(d_rows.reshape(peer_count, slot_depth, model_width))
        summed = lax.psum_scatter(
            contract_first(rows_x, d_both).astype(jnp.bfloat16),
            "dp",
            scatter_dimension=0,
            tiled=True,
        ).astype(jnp.float32)
        gate_parts.append(summed[:, :hidden_units].astype(jnp.bfloat16))
        up_parts.append(summed[:, hidden_units:].astype(jnp.bfloat16))
        down_parts.append(
            lax.psum_scatter(
                contract_first(hidden, d_out).astype(jnp.bfloat16),
                "dp",
                scatter_dimension=0,
                tiled=True,
            )
        )
    grad_gate = jnp.stack(gate_parts)
    grad_up = jnp.stack(up_parts)
    grad_down = jnp.stack(down_parts)
    stacked = jnp.stack(row_list, axis=1)
    returned = lax.all_to_all(stacked, "expert", split_axis=0, concat_axis=0, tiled=True)
    flat_back = returned.reshape(expert_total * slot_depth, model_width)
    row_of_pair = routes.reshape(-1) * slot_depth + slot_rank
    per_pair = flat_back[row_of_pair].astype(jnp.float32).reshape(tok_dev, top_count, model_width)
    grad_tokens = jnp.sum(per_pair, axis=1).astype(jnp.bfloat16)
    return (grad_tokens, grad_gate, grad_up, grad_down)


def pack_kernel(tok_ref, dy_ref, routes_ref, combine_ref, out_ref):
    tok_dev, width = tok_ref.shape
    half = tok_dev // 2
    out_ref[:, :width] = tok_ref[...]
    out_ref[:, width : 2 * width] = dy_ref[...]
    ids = lax.broadcasted_iota(jnp.int32, (half, tok_dev), 0)
    weight = jnp.zeros((half, tok_dev), jnp.float32)
    named = jnp.zeros((half, tok_dev), jnp.float32)
    for k in range(routes_ref.shape[0]):
        hit = routes_ref[k : k + 1, :] == ids
        weight = jnp.where(hit, combine_ref[k : k + 1, :].astype(jnp.float32), weight)
        named = jnp.where(hit, 1.0, named)
    earlier = lax.broadcasted_iota(jnp.int32, (tok_dev, tok_dev), 0) < lax.broadcasted_iota(
        jnp.int32, (tok_dev, tok_dev), 1
    )
    rank = mul(named.astype(jnp.bfloat16), earlier.astype(jnp.bfloat16))
    rank = jnp.where(named > 0.0, rank, -1.0)
    out_ref[:, 2 * width :] = jnp.concatenate([weight, rank], axis=0).astype(jnp.bfloat16)


def pack(tokens, grad_out, routes, combine):
    tok_dev, width = tokens.shape
    return pl.pallas_call(
        pack_kernel,
        out_shape=jax.ShapeDtypeStruct((tok_dev, 2 * width + tok_dev), jnp.bfloat16),
        compiler_params=pltpu.CompilerParams(vmem_limit_bytes=60 * 1024 * 1024),
        cost_estimate=pl.CostEstimate(flops=10**7, bytes_accessed=2 * 10**6, transcendentals=0),
    )(tokens, grad_out, routes.T, combine.T)


def group_kernel(first, last, own, depth, blocks, *refs):
    refs = list(refs)

    def take(count):
        return [refs.pop(0) for _ in range(count)]

    block_hbm = take(blocks)
    gate_ref, up_ref, down_ref = take(3)
    acc_refs = [] if first else take(3)
    out_refs = take(3)
    piece_hbm = take(2) if own else []
    block_buf, x_rows, d_rows, hid, both, info = take(6)
    final_buf = take(3) if last else []
    if own:
        back, places, *piece_buf = take(4)
    block_sem, out_sem, piece_sem = take(3)
    held, rows, width = x_rows.shape
    tok_dev = block_buf.shape[1]
    half = tok_dev // 2
    units = hid.shape[1]
    shard = lax.axis_index("dp")
    base = lax.axis_index("expert") * held
    x_cut = out_refs[0].shape[1]
    h_cut = out_refs[2].shape[1]

    def grad_out(e, m):
        return pltpu.make_async_copy(final_buf[m].at[e], out_refs[m].at[e], out_sem.at[m, e])

    for b in range(blocks):
        pltpu.make_async_copy(block_hbm[b], block_buf.at[b], block_sem.at[b]).start()

    slot = lax.broadcasted_iota(jnp.int32, (depth, tok_dev), 0).astype(jnp.float32)

    def select(b, _):
        pltpu.make_async_copy(block_hbm[0], block_buf.at[b], block_sem.at[b]).wait()
        info[...] = block_buf[b, :, 2 * width :].astype(jnp.float32)
        picks, scaled = [], []
        for i in range(held):
            weight = info[pl.ds(base + i, 1), :]
            rank = info[pl.ds(half + base + i, 1), :]
            hit = slot == rank
            picks.append(jnp.where(hit, 1.0, 0.0))
            scaled.append(jnp.where(hit, weight, 0.0))
        pick = jnp.concatenate(picks, axis=0).astype(jnp.bfloat16)
        scale = jnp.concatenate(scaled, axis=0).astype(jnp.bfloat16)
        if own:

            @pl.when(b < own)
            def _():
                places[b] = pick

        got_x = mul(pick, block_buf[b, :, :width]).astype(jnp.bfloat16)
        got_d = mul(scale, block_buf[b, :, width : 2 * width]).astype(jnp.bfloat16)
        at = pl.ds(pl.multiple_of(b * depth, depth), depth)
        for i in range(held):
            x_rows[i, at, :] = got_x[i * depth : (i + 1) * depth]
            d_rows[i, at, :] = got_d[i * depth : (i + 1) * depth]
        return 0

    lax.fori_loop(0, blocks, select, 0)

    def expert(e, _):
        rows_x = x_rows[e]
        d_out = d_rows[e]
        gate_pre = mul(rows_x, gate_ref[e])
        up_pre = mul(rows_x, up_ref[e])
        d_hidden = contract_last(d_out, down_ref[e])
        sig = 0.5 * jnp.tanh(0.5 * gate_pre) + 0.5
        act = gate_pre * sig
        hid[...] = (act * up_pre).astype(jnp.bfloat16)
        both[:, :units] = (d_hidden * up_pre * (sig + act * (1.0 - sig))).astype(jnp.bfloat16)
        both[:, units:] = (d_hidden * act).astype(jnp.bfloat16)
        x_part = x_rows[e, :, pl.ds(pl.multiple_of(shard * x_cut, LANES), x_cut)]
        h_part = hid[:, pl.ds(pl.multiple_of(shard * h_cut, LANES), h_cut)]
        grad_both = contract_first(x_part, both[...])
        grads = [grad_both[:, :units], grad_both[:, units:], contract_first(h_part, d_out)]
        for m in range(3):
            grad = grads[m] if first else acc_refs[m][e] + grads[m]
            if last:
                final_buf[m][e] = grad.astype(jnp.bfloat16)
                grad_out(e, m).start()
            else:
                out_refs[m][e] = grad
        if own:
            kept = own * depth
            back[e] = (
                contract_last(both[:kept, :units], gate_ref[e])
                + contract_last(both[:kept, units:], up_ref[e])
            ).astype(jnp.bfloat16)
        return 0

    lax.fori_loop(0, held, expert, 0)

    if own:

        def piece_out(odd, p):
            return pltpu.make_async_copy(
                piece_buf[odd].at[p], piece_hbm[odd].at[p], piece_sem.at[odd, p]
            )

        def collect(p, _):
            for odd in range(2):
                at = pl.ds(pl.multiple_of((2 * p + odd) * depth, depth), depth)
                rows_b = jnp.concatenate([back[i, at, :] for i in range(held)], axis=0)
                piece_buf[odd][p] = contract_first(places[2 * p + odd], rows_b).astype(
                    jnp.bfloat16
                )
                piece_out(odd, p).start()
            return 0

        lax.fori_loop(0, own // 2, collect, 0)
        for p in range(own // 2):
            for odd in range(2):
                piece_out(odd, p).wait()
    if last:
        for e in range(held):
            for m in range(3):
                grad_out(e, m).wait()


def group(records, weights, accs, shards, depth, last=False, own=0):
    tok_dev, record = records[0].shape
    held, width, units = weights[0].shape
    blocks = len(records)
    rows = blocks * depth
    first = accs is None
    grad_shapes = [
        (held, width // shards, units),
        (held, width // shards, units),
        (held, units // shards, width),
    ]
    args = list(records) + list(weights) + ([] if first else list(accs))
    out_type = jnp.bfloat16 if last else jnp.float32
    holder = jax.ShapeDtypeStruct if last else pltpu.VMEM
    out_shape = [holder(s, out_type) for s in grad_shapes]
    scratch = [
        pltpu.VMEM((blocks, tok_dev, record), jnp.bfloat16),
        pltpu.VMEM((held, rows, width), jnp.bfloat16),
        pltpu.VMEM((held, rows, width), jnp.bfloat16),
        pltpu.VMEM((rows, units), jnp.bfloat16),
        pltpu.VMEM((rows, 2 * units), jnp.bfloat16),
        pltpu.VMEM((tok_dev, tok_dev), jnp.float32),
    ]
    if last:
        scratch += [pltpu.VMEM(s, jnp.bfloat16) for s in grad_shapes]
    if own:
        piece = (own // 2, tok_dev, width)
        out_shape += [jax.ShapeDtypeStruct(piece, jnp.bfloat16)] * 2
        scratch += [
            pltpu.VMEM((held, own * depth, width), jnp.bfloat16),
            pltpu.VMEM((own, held * depth, tok_dev), jnp.bfloat16),
            pltpu.VMEM(piece, jnp.bfloat16),
            pltpu.VMEM(piece, jnp.bfloat16),
        ]
    scratch += [
        pltpu.SemaphoreType.DMA((blocks,)),
        pltpu.SemaphoreType.DMA((3, held)),
        pltpu.SemaphoreType.DMA((2, max(own // 2, 1))),
    ]
    outside = pl.BlockSpec(memory_space=pltpu.HBM)
    inside = pl.BlockSpec(memory_space=pltpu.VMEM)
    work = 2 * rows * held * width * units
    return pl.pallas_call(
        functools.partial(group_kernel, first, last, own, depth, blocks),
        in_specs=[outside] * blocks + [inside] * (len(args) - blocks),
        out_specs=[outside if last else inside] * 3 + [outside] * (len(out_shape) - 3),
        input_output_aliases={} if first or last else {blocks + 3 + m: m for m in range(3)},
        out_shape=out_shape,
        scratch_shapes=scratch,
        compiler_params=pltpu.CompilerParams(vmem_limit_bytes=VMEM_BYTES),
        cost_estimate=pl.CostEstimate(
            flops=work // 8,
            bytes_accessed=tok_dev * record * 2,
            transcendentals=rows * held * units,
        ),
    )(*args)


def hold_kernel(*refs):
    sem = refs[-1]
    count = len(refs) // 2
    copies = [
        pltpu.make_async_copy(refs[m], refs[count + m], sem.at[m]) for m in range(count)
    ]
    for copy in copies:
        copy.start()
    for copy in copies:
        copy.wait()


def hold(*arrays):
    return pl.pallas_call(
        hold_kernel,
        in_specs=[pl.BlockSpec(memory_space=pl.ANY)] * len(arrays),
        out_specs=[pl.BlockSpec(memory_space=pltpu.VMEM)] * len(arrays),
        out_shape=[pltpu.VMEM(a.shape, a.dtype) for a in arrays],
        scratch_shapes=[pltpu.SemaphoreType.DMA((len(arrays),))],
        compiler_params=pltpu.CompilerParams(vmem_limit_bytes=2 * VMEM_BYTES),
        cost_estimate=pl.CostEstimate(flops=0, bytes_accessed=2 * 10**6, transcendentals=0),
    )(*arrays)


def choose_kernel(inner_ref, outer_ref, out_ref, sem):
    place = lax.axis_index("dp")
    inner = jnp.logical_and(place > 0, place < lax.axis_size("dp") - 1)

    @pl.when(inner)
    def _():
        copy = pltpu.make_async_copy(inner_ref, out_ref, sem)
        copy.start()
        copy.wait()

    @pl.when(jnp.logical_not(inner))
    def _():
        copy = pltpu.make_async_copy(outer_ref, out_ref, sem)
        copy.start()
        copy.wait()


def choose(inner, outer):
    return pl.pallas_call(
        choose_kernel,
        in_specs=[pl.BlockSpec(memory_space=pltpu.HBM)] * 2,
        out_specs=pl.BlockSpec(memory_space=pltpu.HBM),
        out_shape=pltpu.HBM(inner.shape, inner.dtype),
        scratch_shapes=[pltpu.SemaphoreType.DMA],
        compiler_params=pltpu.CompilerParams(vmem_limit_bytes=VMEM_BYTES),
        cost_estimate=pl.CostEstimate(flops=0, bytes_accessed=10**6, transcendentals=0),
    )(inner, outer)


def swap(value, axis, bit):
    size = lax.axis_size(axis)
    return lax.ppermute(value, axis, [(i, i ^ bit) for i in range(size)])


def beside(value):
    return swap(value, "expert", 2)


def below(value):
    return swap(value, "expert", 4)


def pairs(*blocks):
    return [piece for block in blocks for piece in (block, swap(block, "expert", 1))]


def middle(value):
    return lax.ppermute(value, "dp", [(1, 2), (2, 1)])


def outward(value):
    return lax.ppermute(value, "dp", [(1, 0), (2, 3)])


def gathered_shards(tokens, grad_out, routes, combine, w_gate, w_up, w_down):
    shards = lax.axis_size("dp")
    tok_dev = tokens.shape[0]
    depth = depth_of(tok_dev, routes.shape[1], w_gate.shape[0] * lax.axis_size("expert"))
    tie = lax.optimization_barrier
    o0 = pack(tokens, grad_out, routes, combine)
    x0, y0, o1, near = beside(o0), below(o0), swap(o0, "dp", 1), middle(o0)
    group0 = pairs(o0)
    weights = hold(*tie((w_gate, w_up, w_down, o0))[:3])
    x0, y0, o1, near, group0, weights = tie((x0, y0, o1, near, group0, weights))
    run = functools.partial(group, weights=weights, shards=shards, depth=depth)
    x1, d0, near_end, far = beside(o1), below(x0), outward(near), middle(o1)
    group0 += pairs(x0, y0, o1)
    y0, near, group0 = tie((y0, near, group0))
    *accs, even0, odd0 = run(group0, accs=None, own=6)
    x1, d0, near_end, near, far, even0, odd0, y0 = tie(
        (x1, d0, near_end, near, far, even0, odd0, y0)
    )
    o2 = choose(near, near_end)
    x2, y2, far_end = beside(o2), below(o2), outward(far)
    crossed0 = swap(odd0, "expert", 1)
    group1 = pairs(d0, x1, o2)
    pair0 = (even0.astype(jnp.float32) + crossed0.astype(jnp.float32)).astype(jnp.bfloat16)
    group1, pair0, d0 = tie((group1, pair0, d0))
    sent = [beside(pair0[1]), below(pair0[2])]
    *accs, even1, odd1 = run(group1, accs=accs, own=2)
    x2, y2, far_end, y0, far, d0, even1, odd1, sent = tie(
        (x2, y2, far_end, y0, far, d0, even1, odd1, sent)
    )
    o3 = choose(far, far_end)
    x3, y3, y1 = beside(o3), below(o3), swap(y0, "dp", 1)
    crossed1 = swap(odd1, "expert", 1)
    group2 = pairs(x2, y2, o3)
    group2, crossed1 = tie((group2, crossed1))
    pair1 = (even1.astype(jnp.float32) + crossed1.astype(jnp.float32)).astype(jnp.bfloat16)
    accs = run(group2, accs=accs)
    x3, y3, y1, accs, pair1, d0, x2 = tie((x3, y3, y1, accs, pair1, d0, x2))
    d3, d2, d1 = beside(y3), below(x2), swap(d0, "dp", 1)
    accs = run(pairs(x3, y3, y1), accs=accs)
    d3, d2, d1, accs, pair1 = tie((d3, d2, d1, accs, pair1))
    sent.append(swap(pair1[0], "expert", 6))
    accs = run(pairs(d1, d2, d3), accs=accs, last=True)
    sent, accs = tie((sent, accs))
    total = pair0[0].astype(jnp.float32)
    for piece in sent:
        total = total + piece.astype(jnp.float32)
    return (total.astype(jnp.bfloat16), *accs)


def solution(mesh):
    shards, peers = mesh.shape["dp"], mesh.shape["expert"]

    def body(tokens, grad_out, routes, combine, w_gate, w_up, w_down):
        tok_dev, width = tokens.shape
        gathered = shards * peers * tok_dev * (2 * width + tok_dev) * 2
        fits = (
            peers == 8
            and shards == 4
            and peers * w_gate.shape[0] <= tok_dev // 2
            and tok_dev == LANES
            and gathered <= GATHER_BYTES
        )
        plan = gathered_shards if fits else routed_shards
        return plan(tokens, grad_out, routes, combine, w_gate, w_up, w_down)

    return jax.shard_map(
        body,
        mesh=mesh,
        in_specs=(
            P(("dp", "expert"), None),
            P(("dp", "expert"), None),
            P(("dp", "expert"), None),
            P(("dp", "expert"), None),
            P("expert", None, None),
            P("expert", None, None),
            P("expert", None, None),
        ),
        out_specs=(
            P(("dp", "expert"), None),
            P("expert", "dp", None),
            P("expert", "dp", None),
            P("expert", "dp", None),
        ),
        check_vma=False,
    )
```

```python
import functools
import jax
import jax.numpy as jnp
from jax import lax
from jax.experimental import pallas as pl
from jax.experimental.pallas import tpu as pltpu
from jax.sharding import PartitionSpec as P

LANES = 128
VMEM_BYTES = 26 * 1024 * 1024
GATHER_BYTES = 48 * 1024 * 1024


def slot_ranks(route_block, expert_total):
    flat_ids = route_block.reshape(-1)
    marks = (flat_ids[:, None] == jnp.arange(expert_total, dtype=jnp.int32)[None, :]).astype(
        jnp.int32
    )
    return jnp.sum((jnp.cumsum(marks, axis=0) - 1) * marks, axis=1)


def build_slots(route_block, expert_total, slot_depth):
    flat_ids = route_block.reshape(-1)
    pair_total = flat_ids.shape[0]
    slot_rank = slot_ranks(route_block, expert_total)
    slots = jnp.full((expert_total, slot_depth), pair_total, dtype=jnp.int32)
    slots = slots.at[flat_ids, slot_rank].set(jnp.arange(pair_total, dtype=jnp.int32))
    return (slots, slot_rank)


def contract_last(left, right):
    return lax.dot_general(
        left, right, (((1,), (1,)), ((), ())), preferred_element_type=jnp.float32
    )


def contract_first(left, right):
    return lax.dot_general(
        left, right, (((0,), (0,)), ((), ())), preferred_element_type=jnp.float32
    )


def mul(left, right):
    return jnp.dot(left, right, preferred_element_type=jnp.float32)


def depth_of(tok_dev, top_count, expert_total):
    return 8 * ((tok_dev * top_count * 6 // (5 * expert_total) + 7) // 8)


def expert_backward(rows_x, rows_dy, rows_c, gate_w, up_w, down_w):
    gate_pre = mul(rows_x, gate_w)
    up_pre = mul(rows_x, up_w)
    sigmoid_gate = jax.nn.sigmoid(gate_pre)
    hidden = (gate_pre * sigmoid_gate * up_pre).astype(jnp.bfloat16)
    d_out = (rows_c[:, None] * rows_dy.astype(jnp.float32)).astype(jnp.bfloat16)
    d_hidden = contract_last(d_out, down_w)
    d_gate = (d_hidden * up_pre * sigmoid_gate * (1.0 + gate_pre * (1.0 - sigmoid_gate))).astype(
        jnp.bfloat16
    )
    d_up = (d_hidden * gate_pre * sigmoid_gate).astype(jnp.bfloat16)
    d_rows = (contract_last(d_gate, gate_w) + contract_last(d_up, up_w)).astype(jnp.bfloat16)
    return (hidden, d_out, d_gate, d_up, d_rows)


def routed_shards(tokens, grad_out, routes, combine, w_gate, w_up, w_down):
    tok_dev, model_width = tokens.shape
    top_count = routes.shape[1]
    peer_count = lax.axis_size("expert")
    held_experts = w_gate.shape[0]
    hidden_units = w_gate.shape[2]
    expert_total = peer_count * held_experts
    slot_depth = depth_of(tok_dev, top_count, expert_total)
    pair_total = tok_dev * top_count
    slots, slot_rank = build_slots(routes, expert_total, slot_depth)
    filled = slots < pair_total
    token_index = jnp.where(filled, slots // top_count, tok_dev)
    pad_row = jnp.zeros((1, model_width), jnp.bfloat16)
    send_x = jnp.concatenate([tokens, pad_row])[token_index].reshape(
        peer_count, held_experts, slot_depth, model_width
    )
    send_dy = jnp.concatenate([grad_out, pad_row])[token_index].reshape(
        peer_count, held_experts, slot_depth, model_width
    )
    weight_ext = jnp.concatenate([combine.reshape(-1), jnp.zeros((1,), jnp.bfloat16)])
    send_c = weight_ext[slots].reshape(peer_count, held_experts, slot_depth)
    recv_x, recv_dy, recv_c = (
        lax.all_to_all(send_x, "expert", split_axis=0, concat_axis=0, tiled=True),
        lax.all_to_all(send_dy, "expert", split_axis=0, concat_axis=0, tiled=True),
        lax.all_to_all(send_c, "expert", split_axis=0, concat_axis=0, tiled=True),
    )
    gate_parts = []
    up_parts = []
    down_parts = []
    row_list = []
    for which in range(held_experts):
        rows_x = recv_x[:, which].reshape(-1, model_width)
        rows_dy = recv_dy[:, which].reshape(-1, model_width)
        rows_c = recv_c[:, which].reshape(-1).astype(jnp.float32)
        hidden, d_out, d_gate, d_up, d_rows = expert_backward(
            rows_x, rows_dy, rows_c, w_gate[which], w_up[which], w_down[which]
        )
        d_both = jnp.concatenate([d_gate, d_up], axis=1)
        row_list.append(d_rows.reshape(peer_count, slot_depth, model_width))
        summed = lax.psum_scatter(
            contract_first(rows_x, d_both).astype(jnp.bfloat16),
            "dp",
            scatter_dimension=0,
            tiled=True,
        ).astype(jnp.float32)
        gate_parts.append(summed[:, :hidden_units].astype(jnp.bfloat16))
        up_parts.append(summed[:, hidden_units:].astype(jnp.bfloat16))
        down_parts.append(
            lax.psum_scatter(
                contract_first(hidden, d_out).astype(jnp.bfloat16),
                "dp",
                scatter_dimension=0,
                tiled=True,
            )
        )
    grad_gate = jnp.stack(gate_parts)
    grad_up = jnp.stack(up_parts)
    grad_down = jnp.stack(down_parts)
    stacked = jnp.stack(row_list, axis=1)
    returned = lax.all_to_all(stacked, "expert", split_axis=0, concat_axis=0, tiled=True)
    flat_back = returned.reshape(expert_total * slot_depth, model_width)
    row_of_pair = routes.reshape(-1) * slot_depth + slot_rank
    per_pair = flat_back[row_of_pair].astype(jnp.float32).reshape(tok_dev, top_count, model_width)
    grad_tokens = jnp.sum(per_pair, axis=1).astype(jnp.bfloat16)
    return (grad_tokens, grad_gate, grad_up, grad_down)


def pack_kernel(tok_ref, dy_ref, routes_ref, combine_ref, out_ref):
    tok_dev, width = tok_ref.shape
    half = tok_dev // 2
    out_ref[:, :width] = tok_ref[...]
    out_ref[:, width : 2 * width] = dy_ref[...]
    ids = lax.broadcasted_iota(jnp.int32, (half, tok_dev), 0)
    weight = jnp.zeros((half, tok_dev), jnp.float32)
    named = jnp.zeros((half, tok_dev), jnp.float32)
    for k in range(routes_ref.shape[0]):
        hit = routes_ref[k : k + 1, :] == ids
        weight = jnp.where(hit, combine_ref[k : k + 1, :].astype(jnp.float32), weight)
        named = jnp.where(hit, 1.0, named)
    earlier = lax.broadcasted_iota(jnp.int32, (tok_dev, tok_dev), 0) < lax.broadcasted_iota(
        jnp.int32, (tok_dev, tok_dev), 1
    )
    rank = mul(named.astype(jnp.bfloat16), earlier.astype(jnp.bfloat16))
    rank = jnp.where(named > 0.0, rank, -1.0)
    out_ref[:, 2 * width :] = jnp.concatenate([weight, rank], axis=0).astype(jnp.bfloat16)


def pack(tokens, grad_out, routes, combine):
    tok_dev, width = tokens.shape
    return pl.pallas_call(
        pack_kernel,
        out_shape=jax.ShapeDtypeStruct((tok_dev, 2 * width + tok_dev), jnp.bfloat16),
        compiler_params=pltpu.CompilerParams(vmem_limit_bytes=60 * 1024 * 1024),
        cost_estimate=pl.CostEstimate(flops=10**7, bytes_accessed=2 * 10**6, transcendentals=0),
    )(tokens, grad_out, routes.T, combine.T)


def group_kernel(first, last, own, depth, blocks, *refs):
    refs = list(refs)

    def take(count):
        return [refs.pop(0) for _ in range(count)]

    block_hbm = take(blocks)
    gate_ref, up_ref, across_ref = take(3)
    acc_refs = [] if first else take(3)
    out_refs = take(3)
    piece_hbm = take(2) if own else []
    block_buf, x_rows, d_rows, hid, both, info = take(6)
    final_buf = take(3) if last else []
    if own:
        back, places, *piece_buf = take(4)
    block_sem, out_sem, piece_sem = take(3)
    held, rows, width = x_rows.shape
    tok_dev = block_buf.shape[1]
    half = tok_dev // 2
    units = hid.shape[1]
    shard = lax.axis_index("dp")
    base = lax.axis_index("expert") * held
    x_cut = out_refs[0].shape[1]
    h_cut = out_refs[2].shape[1]

    def grad_out(e, m):
        return pltpu.make_async_copy(final_buf[m].at[e], out_refs[m].at[e], out_sem.at[m, e])

    for b in range(blocks):
        pltpu.make_async_copy(block_hbm[b], block_buf.at[b], block_sem.at[b]).start()

    slot = lax.broadcasted_iota(jnp.int32, (depth, tok_dev), 0).astype(jnp.float32)

    def select(b, _):
        pltpu.make_async_copy(block_hbm[0], block_buf.at[b], block_sem.at[b]).wait()
        info[...] = block_buf[b, :, 2 * width :].astype(jnp.float32)
        picks, scaled = [], []
        for i in range(held):
            weight = info[pl.ds(base + i, 1), :]
            rank = info[pl.ds(half + base + i, 1), :]
            hit = slot == rank
            picks.append(jnp.where(hit, 1.0, 0.0))
            scaled.append(jnp.where(hit, weight, 0.0))
        pick = jnp.concatenate(picks, axis=0).astype(jnp.bfloat16)
        scale = jnp.concatenate(scaled, axis=0).astype(jnp.bfloat16)
        if own:

            @pl.when(b < own)
            def _():
                places[b] = pick

        got_x = mul(pick, block_buf[b, :, :width]).astype(jnp.bfloat16)
        got_d = mul(scale, block_buf[b, :, width : 2 * width]).astype(jnp.bfloat16)
        at = pl.ds(pl.multiple_of(b * depth, depth), depth)
        for i in range(held):
            x_rows[i, at, :] = got_x[i * depth : (i + 1) * depth]
            d_rows[i, at, :] = got_d[i * depth : (i + 1) * depth]
        return 0

    lax.fori_loop(0, blocks, select, 0)

    def expert(e, _):
        rows_x = x_rows[e]
        d_out = d_rows[e]
        gate_pre = mul(rows_x, gate_ref[e])
        up_pre = mul(rows_x, up_ref[e])
        d_hidden = mul(d_out, across_ref[e])
        sig = 0.5 * jnp.tanh(0.5 * gate_pre) + 0.5
        act = gate_pre * sig
        hid[...] = (act * up_pre).astype(jnp.bfloat16)
        both[:, :units] = (d_hidden * up_pre * (sig + act * (1.0 - sig))).astype(jnp.bfloat16)
        both[:, units:] = (d_hidden * act).astype(jnp.bfloat16)
        x_part = x_rows[e, :, pl.ds(pl.multiple_of(shard * x_cut, LANES), x_cut)]
        h_part = hid[:, pl.ds(pl.multiple_of(shard * h_cut, LANES), h_cut)]
        grad_both = contract_first(x_part, both[...])
        grads = [grad_both[:, :units], grad_both[:, units:], contract_first(h_part, d_out)]
        for m in range(3):
            grad = grads[m] if first else acc_refs[m][e] + grads[m]
            if last:
                final_buf[m][e] = grad.astype(jnp.bfloat16)
                grad_out(e, m).start()
            else:
                out_refs[m][e] = grad
        if own:
            kept = own * depth
            back[e] = (
                contract_last(both[:kept, :units], gate_ref[e])
                + contract_last(both[:kept, units:], up_ref[e])
            ).astype(jnp.bfloat16)
        return 0

    lax.fori_loop(0, held, expert, 0)

    if own:

        def piece_out(odd, p):
            return pltpu.make_async_copy(
                piece_buf[odd].at[p], piece_hbm[odd].at[p], piece_sem.at[odd, p]
            )

        def collect(p, _):
            for odd in range(2):
                at = pl.ds(pl.multiple_of((2 * p + odd) * depth, depth), depth)
                rows_b = jnp.concatenate([back[i, at, :] for i in range(held)], axis=0)
                piece_buf[odd][p] = contract_first(places[2 * p + odd], rows_b).astype(
                    jnp.bfloat16
                )
                piece_out(odd, p).start()
            return 0

        lax.fori_loop(0, own // 2, collect, 0)
        for p in range(own // 2):
            for odd in range(2):
                piece_out(odd, p).wait()
    if last:
        for e in range(held):
            for m in range(3):
                grad_out(e, m).wait()


def group(records, weights, accs, shards, depth, last=False, own=0):
    tok_dev, record = records[0].shape
    held, width, units = weights[0].shape
    blocks = len(records)
    rows = blocks * depth
    first = accs is None
    grad_shapes = [
        (held, width // shards, units),
        (held, width // shards, units),
        (held, units // shards, width),
    ]
    args = list(records) + list(weights) + ([] if first else list(accs))
    out_type = jnp.bfloat16 if last else jnp.float32
    holder = jax.ShapeDtypeStruct if last else pltpu.VMEM
    out_shape = [holder(s, out_type) for s in grad_shapes]
    scratch = [
        pltpu.VMEM((blocks, tok_dev, record), jnp.bfloat16),
        pltpu.VMEM((held, rows, width), jnp.bfloat16),
        pltpu.VMEM((held, rows, width), jnp.bfloat16),
        pltpu.VMEM((rows, units), jnp.bfloat16),
        pltpu.VMEM((rows, 2 * units), jnp.bfloat16),
        pltpu.VMEM((tok_dev, tok_dev), jnp.float32),
    ]
    if last:
        scratch += [pltpu.VMEM(s, jnp.bfloat16) for s in grad_shapes]
    if own:
        piece = (own // 2, tok_dev, width)
        out_shape += [jax.ShapeDtypeStruct(piece, jnp.bfloat16)] * 2
        scratch += [
            pltpu.VMEM((held, own * depth, width), jnp.bfloat16),
            pltpu.VMEM((own, held * depth, tok_dev), jnp.bfloat16),
            pltpu.VMEM(piece, jnp.bfloat16),
            pltpu.VMEM(piece, jnp.bfloat16),
        ]
    scratch += [
        pltpu.SemaphoreType.DMA((blocks,)),
        pltpu.SemaphoreType.DMA((3, held)),
        pltpu.SemaphoreType.DMA((2, max(own // 2, 1))),
    ]
    outside = pl.BlockSpec(memory_space=pltpu.HBM)
    inside = pl.BlockSpec(memory_space=pltpu.VMEM)
    work = 2 * rows * held * width * units
    return pl.pallas_call(
        functools.partial(group_kernel, first, last, own, depth, blocks),
        in_specs=[outside] * blocks + [inside] * (len(args) - blocks),
        out_specs=[outside if last else inside] * 3 + [outside] * (len(out_shape) - 3),
        input_output_aliases={} if first or last else {blocks + 3 + m: m for m in range(3)},
        out_shape=out_shape,
        scratch_shapes=scratch,
        compiler_params=pltpu.CompilerParams(vmem_limit_bytes=VMEM_BYTES),
        cost_estimate=pl.CostEstimate(
            flops=work // 8,
            bytes_accessed=tok_dev * record * 2,
            transcendentals=rows * held * units,
        ),
    )(*args)


def hold_kernel(gate_hbm, up_hbm, down_hbm, gate_ref, up_ref, across_ref, down_buf, sem):
    held, units, _ = down_buf.shape
    refs = ((down_hbm, down_buf), (gate_hbm, gate_ref), (up_hbm, up_ref))
    copies = [pltpu.make_async_copy(a, b, sem.at[m]) for m, (a, b) in enumerate(refs)]
    for copy in copies:
        copy.start()
    copies[0].wait()

    def turn(e, _):
        for at in range(0, units, LANES):
            cut = slice(at, at + LANES)
            across_ref[e, :, cut] = down_buf[e, cut, :].T
        return 0

    lax.fori_loop(0, held, turn, 0)
    for copy in copies[1:]:
        copy.wait()


def hold(w_gate, w_up, w_down):
    held, units, width = w_down.shape
    shapes = [w_gate.shape, w_up.shape, (held, width, units)]
    return pl.pallas_call(
        hold_kernel,
        in_specs=[pl.BlockSpec(memory_space=pl.ANY)] * 3,
        out_specs=[pl.BlockSpec(memory_space=pltpu.VMEM)] * 3,
        out_shape=[pltpu.VMEM(s, w_down.dtype) for s in shapes],
        scratch_shapes=[pltpu.VMEM(w_down.shape, w_down.dtype), pltpu.SemaphoreType.DMA((3,))],
        compiler_params=pltpu.CompilerParams(vmem_limit_bytes=2 * VMEM_BYTES),
        cost_estimate=pl.CostEstimate(flops=0, bytes_accessed=2 * 10**6, transcendentals=0),
    )(w_gate, w_up, w_down)


def choose_kernel(inner_ref, outer_ref, out_ref, buf, sem):
    place = lax.axis_index("dp")
    inner = jnp.logical_and(place > 0, place < lax.axis_size("dp") - 1)

    def move(source, target):
        copy = pltpu.make_async_copy(source, target, sem)
        copy.start()
        copy.wait()

    @pl.when(inner)
    def _():
        move(inner_ref, buf)

    @pl.when(jnp.logical_not(inner))
    def _():
        move(outer_ref, buf)

    move(buf, out_ref)


def choose(inner, outer):
    return pl.pallas_call(
        choose_kernel,
        in_specs=[pl.BlockSpec(memory_space=pl.ANY)] * 2,
        out_specs=pl.BlockSpec(memory_space=pltpu.HBM),
        out_shape=pltpu.HBM(inner.shape, inner.dtype),
        scratch_shapes=[pltpu.VMEM(inner.shape, inner.dtype), pltpu.SemaphoreType.DMA],
        compiler_params=pltpu.CompilerParams(vmem_limit_bytes=VMEM_BYTES),
        cost_estimate=pl.CostEstimate(flops=0, bytes_accessed=10**6, transcendentals=0),
    )(inner, outer)


def swap(value, axis, bit):
    size = lax.axis_size(axis)
    return lax.ppermute(value, axis, [(i, i ^ bit) for i in range(size)])


def beside(value):
    return swap(value, "expert", 2)


def below(value):
    return swap(value, "expert", 4)


def pairs(*blocks):
    return [piece for block in blocks for piece in (block, swap(block, "expert", 1))]


def middle(value):
    return lax.ppermute(value, "dp", [(1, 2), (2, 1)])


def outward(value):
    return lax.ppermute(value, "dp", [(1, 0), (2, 3)])


def gathered_shards(tokens, grad_out, routes, combine, w_gate, w_up, w_down):
    shards = lax.axis_size("dp")
    tok_dev = tokens.shape[0]
    depth = depth_of(tok_dev, routes.shape[1], w_gate.shape[0] * lax.axis_size("expert"))
    tie = lax.optimization_barrier
    o0 = pack(tokens, grad_out, routes, combine)
    near, o1, x0, y0 = middle(o0), swap(o0, "dp", 1), beside(o0), below(o0)
    group0 = pairs(o0)
    weights = hold(*tie((w_gate, w_up, w_down, o0))[:3])
    run = functools.partial(group, weights=weights, shards=shards, depth=depth)
    *accs, mine, theirs = run(group0, accs=None, own=2)
    near, o1, x0, y0, accs, theirs = tie((near, o1, x0, y0, accs, theirs))
    near_end, far, d0, x1 = outward(near), middle(o1), below(x0), beside(o1)
    group0 = pairs(x0, y0, o1)
    y0, near, group0, accs = tie((y0, near, group0, accs))
    *accs, even0, odd0 = run(group0, accs=accs, own=4)
    near_end, near, even0, odd0 = tie((near_end, near, even0, odd0))
    o2 = choose(near, near_end)
    far, d0, x1, o2, y0, odd0 = tie((far, d0, x1, o2, y0, odd0))
    x2, y2, far_end = beside(o2), below(o2), outward(far)
    crossed0 = swap(odd0, "expert", 1)
    group1 = pairs(d0, x1, o2)
    pair0 = (even0.astype(jnp.float32) + crossed0.astype(jnp.float32)).astype(jnp.bfloat16)
    group1, pair0, d0 = tie((group1, pair0, d0))
    sent = [beside(pair0[0]), below(pair0[1])]
    *accs, even1, odd1 = run(group1, accs=accs, own=2)
    far_end, far, even1, odd1 = tie((far_end, far, even1, odd1))
    o3 = choose(far, far_end)
    x2, y2, y0, o3, d0, odd1, sent = tie((x2, y2, y0, o3, d0, odd1, sent))
    x3, y3, y1 = beside(o3), below(o3), swap(y0, "dp", 1)
    crossed1 = swap(odd1, "expert", 1)
    group2 = pairs(x2, y2, o3)
    group2, crossed1 = tie((group2, crossed1))
    pair1 = (even1.astype(jnp.float32) + crossed1.astype(jnp.float32)).astype(jnp.bfloat16)
    accs = run(group2, accs=accs)
    x3, y3, y1, accs, pair1, d0, x2 = tie((x3, y3, y1, accs, pair1, d0, x2))
    d3, d2, d1 = beside(y3), below(x2), swap(d0, "dp", 1)
    accs = run(pairs(x3, y3, y1), accs=accs)
    d3, d2, d1, accs, pair1, theirs = tie((d3, d2, d1, accs, pair1, theirs))
    sent += [swap(pair1[0], "expert", 6), swap(theirs[0], "expert", 1)]
    accs = run(pairs(d1, d2, d3), accs=accs, last=True)
    sent, accs = tie((sent, accs))
    total = mine[0].astype(jnp.float32)
    for piece in sent:
        total = total + piece.astype(jnp.float32)
    return (total.astype(jnp.bfloat16), *accs)


def solution(mesh):
    shards, peers = mesh.shape["dp"], mesh.shape["expert"]

    def body(tokens, grad_out, routes, combine, w_gate, w_up, w_down):
        tok_dev, width = tokens.shape
        gathered = shards * peers * tok_dev * (2 * width + tok_dev) * 2
        fits = (
            peers == 8
            and shards == 4
            and peers * w_gate.shape[0] <= tok_dev // 2
            and tok_dev == LANES
            and gathered <= GATHER_BYTES
        )
        plan = gathered_shards if fits else routed_shards
        return plan(tokens, grad_out, routes, combine, w_gate, w_up, w_down)

    return jax.shard_map(
        body,
        mesh=mesh,
        in_specs=(
            P(("dp", "expert"), None),
            P(("dp", "expert"), None),
            P(("dp", "expert"), None),
            P(("dp", "expert"), None),
            P("expert", None, None),
            P("expert", None, None),
            P("expert", None, None),
        ),
        out_specs=(
            P(("dp", "expert"), None),
            P("expert", "dp", None),
            P("expert", "dp", None),
            P("expert", "dp", None),
        ),
        check_vma=False,
    )
```

```python
import functools
import jax
import jax.numpy as jnp
from jax import lax
from jax.experimental import pallas as pl
from jax.experimental.pallas import tpu as pltpu
from jax.sharding import PartitionSpec as P

LANES = 128
VMEM_BYTES = 26 * 1024 * 1024
GATHER_BYTES = 48 * 1024 * 1024


def slot_ranks(route_block, expert_total):
    flat_ids = route_block.reshape(-1)
    marks = (flat_ids[:, None] == jnp.arange(expert_total, dtype=jnp.int32)[None, :]).astype(
        jnp.int32
    )
    return jnp.sum((jnp.cumsum(marks, axis=0) - 1) * marks, axis=1)


def build_slots(route_block, expert_total, slot_depth):
    flat_ids = route_block.reshape(-1)
    pair_total = flat_ids.shape[0]
    slot_rank = slot_ranks(route_block, expert_total)
    slots = jnp.full((expert_total, slot_depth), pair_total, dtype=jnp.int32)
    slots = slots.at[flat_ids, slot_rank].set(jnp.arange(pair_total, dtype=jnp.int32))
    return (slots, slot_rank)


def contract_last(left, right):
    return lax.dot_general(
        left, right, (((1,), (1,)), ((), ())), preferred_element_type=jnp.float32
    )


def contract_first(left, right):
    return lax.dot_general(
        left, right, (((0,), (0,)), ((), ())), preferred_element_type=jnp.float32
    )


def mul(left, right):
    return jnp.dot(left, right, preferred_element_type=jnp.float32)


def depth_of(tok_dev, top_count, expert_total):
    return 8 * ((tok_dev * top_count * 6 // (5 * expert_total) + 7) // 8)


def expert_backward(rows_x, rows_dy, rows_c, gate_w, up_w, down_w):
    gate_pre = mul(rows_x, gate_w)
    up_pre = mul(rows_x, up_w)
    sigmoid_gate = jax.nn.sigmoid(gate_pre)
    hidden = (gate_pre * sigmoid_gate * up_pre).astype(jnp.bfloat16)
    d_out = (rows_c[:, None] * rows_dy.astype(jnp.float32)).astype(jnp.bfloat16)
    d_hidden = contract_last(d_out, down_w)
    d_gate = (d_hidden * up_pre * sigmoid_gate * (1.0 + gate_pre * (1.0 - sigmoid_gate))).astype(
        jnp.bfloat16
    )
    d_up = (d_hidden * gate_pre * sigmoid_gate).astype(jnp.bfloat16)
    d_rows = (contract_last(d_gate, gate_w) + contract_last(d_up, up_w)).astype(jnp.bfloat16)
    return (hidden, d_out, d_gate, d_up, d_rows)


def routed_shards(tokens, grad_out, routes, combine, w_gate, w_up, w_down):
    tok_dev, model_width = tokens.shape
    top_count = routes.shape[1]
    peer_count = lax.axis_size("expert")
    held_experts = w_gate.shape[0]
    hidden_units = w_gate.shape[2]
    expert_total = peer_count * held_experts
    slot_depth = depth_of(tok_dev, top_count, expert_total)
    pair_total = tok_dev * top_count
    slots, slot_rank = build_slots(routes, expert_total, slot_depth)
    filled = slots < pair_total
    token_index = jnp.where(filled, slots // top_count, tok_dev)
    pad_row = jnp.zeros((1, model_width), jnp.bfloat16)
    send_x = jnp.concatenate([tokens, pad_row])[token_index].reshape(
        peer_count, held_experts, slot_depth, model_width
    )
    send_dy = jnp.concatenate([grad_out, pad_row])[token_index].reshape(
        peer_count, held_experts, slot_depth, model_width
    )
    weight_ext = jnp.concatenate([combine.reshape(-1), jnp.zeros((1,), jnp.bfloat16)])
    send_c = weight_ext[slots].reshape(peer_count, held_experts, slot_depth)
    recv_x, recv_dy, recv_c = (
        lax.all_to_all(send_x, "expert", split_axis=0, concat_axis=0, tiled=True),
        lax.all_to_all(send_dy, "expert", split_axis=0, concat_axis=0, tiled=True),
        lax.all_to_all(send_c, "expert", split_axis=0, concat_axis=0, tiled=True),
    )
    gate_parts = []
    up_parts = []
    down_parts = []
    row_list = []
    for which in range(held_experts):
        rows_x = recv_x[:, which].reshape(-1, model_width)
        rows_dy = recv_dy[:, which].reshape(-1, model_width)
        rows_c = recv_c[:, which].reshape(-1).astype(jnp.float32)
        hidden, d_out, d_gate, d_up, d_rows = expert_backward(
            rows_x, rows_dy, rows_c, w_gate[which], w_up[which], w_down[which]
        )
        d_both = jnp.concatenate([d_gate, d_up], axis=1)
        row_list.append(d_rows.reshape(peer_count, slot_depth, model_width))
        summed = lax.psum_scatter(
            contract_first(rows_x, d_both).astype(jnp.bfloat16),
            "dp",
            scatter_dimension=0,
            tiled=True,
        ).astype(jnp.float32)
        gate_parts.append(summed[:, :hidden_units].astype(jnp.bfloat16))
        up_parts.append(summed[:, hidden_units:].astype(jnp.bfloat16))
        down_parts.append(
            lax.psum_scatter(
                contract_first(hidden, d_out).astype(jnp.bfloat16),
                "dp",
                scatter_dimension=0,
                tiled=True,
            )
        )
    grad_gate = jnp.stack(gate_parts)
    grad_up = jnp.stack(up_parts)
    grad_down = jnp.stack(down_parts)
    stacked = jnp.stack(row_list, axis=1)
    returned = lax.all_to_all(stacked, "expert", split_axis=0, concat_axis=0, tiled=True)
    flat_back = returned.reshape(expert_total * slot_depth, model_width)
    row_of_pair = routes.reshape(-1) * slot_depth + slot_rank
    per_pair = flat_back[row_of_pair].astype(jnp.float32).reshape(tok_dev, top_count, model_width)
    grad_tokens = jnp.sum(per_pair, axis=1).astype(jnp.bfloat16)
    return (grad_tokens, grad_gate, grad_up, grad_down)


def pack_kernel(tok_ref, dy_ref, routes_ref, combine_ref, out_ref):
    tok_dev, width = tok_ref.shape
    half = tok_dev // 2
    out_ref[:, :width] = tok_ref[...]
    out_ref[:, width : 2 * width] = dy_ref[...]
    ids = lax.broadcasted_iota(jnp.int32, (half, tok_dev), 0)
    weight = jnp.zeros((half, tok_dev), jnp.float32)
    named = jnp.zeros((half, tok_dev), jnp.float32)
    for k in range(routes_ref.shape[0]):
        hit = routes_ref[k : k + 1, :] == ids
        weight = jnp.where(hit, combine_ref[k : k + 1, :].astype(jnp.float32), weight)
        named = jnp.where(hit, 1.0, named)
    earlier = lax.broadcasted_iota(jnp.int32, (tok_dev, tok_dev), 0) < lax.broadcasted_iota(
        jnp.int32, (tok_dev, tok_dev), 1
    )
    rank = mul(named.astype(jnp.bfloat16), earlier.astype(jnp.bfloat16))
    rank = jnp.where(named > 0.0, rank, -1.0)
    out_ref[:, 2 * width :] = jnp.concatenate([weight, rank], axis=0).astype(jnp.bfloat16)


def pack(tokens, grad_out, routes, combine):
    tok_dev, width = tokens.shape
    return pl.pallas_call(
        pack_kernel,
        out_shape=jax.ShapeDtypeStruct((tok_dev, 2 * width + tok_dev), jnp.bfloat16),
        compiler_params=pltpu.CompilerParams(vmem_limit_bytes=60 * 1024 * 1024),
        cost_estimate=pl.CostEstimate(flops=10**7, bytes_accessed=2 * 10**6, transcendentals=0),
    )(tokens, grad_out, routes.T, combine.T)


def group_kernel(first, last, own, depth, blocks, *refs):
    refs = list(refs)

    def take(count):
        return [refs.pop(0) for _ in range(count)]

    block_hbm = take(blocks)
    gate_ref, up_ref, across_ref = take(3)
    acc_refs = [] if first else take(3)
    out_refs = take(3)
    piece_hbm = take(2) if own else []
    block_buf, x_rows, d_rows, hid, both, info = take(6)
    final_buf = take(3) if last else []
    if own:
        back, places, *piece_buf = take(4)
    block_sem, out_sem, piece_sem = take(3)
    held, rows, width = x_rows.shape
    tok_dev = block_buf.shape[1]
    half = tok_dev // 2
    units = hid.shape[1]
    shard = lax.axis_index("dp")
    base = lax.axis_index("expert") * held
    x_cut = out_refs[0].shape[1]
    h_cut = out_refs[2].shape[1]

    def grad_out(e, m):
        return pltpu.make_async_copy(final_buf[m].at[e], out_refs[m].at[e], out_sem.at[m, e])

    for b in range(blocks):
        pltpu.make_async_copy(block_hbm[b], block_buf.at[b], block_sem.at[b]).start()

    slot = lax.broadcasted_iota(jnp.int32, (depth, tok_dev), 0).astype(jnp.float32)

    def select(b, _):
        pltpu.make_async_copy(block_hbm[0], block_buf.at[b], block_sem.at[b]).wait()
        info[...] = block_buf[b, :, 2 * width :].astype(jnp.float32)
        picks, scaled = [], []
        for i in range(held):
            weight = info[pl.ds(base + i, 1), :]
            rank = info[pl.ds(half + base + i, 1), :]
            hit = slot == rank
            picks.append(jnp.where(hit, 1.0, 0.0))
            scaled.append(jnp.where(hit, weight, 0.0))
        pick = jnp.concatenate(picks, axis=0).astype(jnp.bfloat16)
        scale = jnp.concatenate(scaled, axis=0).astype(jnp.bfloat16)
        if own:

            @pl.when(b < own)
            def _():
                places[b] = pick

        got_x = mul(pick, block_buf[b, :, :width]).astype(jnp.bfloat16)
        got_d = mul(scale, block_buf[b, :, width : 2 * width]).astype(jnp.bfloat16)
        at = pl.ds(pl.multiple_of(b * depth, depth), depth)
        for i in range(held):
            x_rows[i, at, :] = got_x[i * depth : (i + 1) * depth]
            d_rows[i, at, :] = got_d[i * depth : (i + 1) * depth]
        return 0

    lax.fori_loop(0, blocks, select, 0)

    def expert(e, _):
        rows_x = x_rows[e]
        d_out = d_rows[e]
        gate_pre = mul(rows_x, gate_ref[e])
        up_pre = mul(rows_x, up_ref[e])
        d_hidden = mul(d_out, across_ref[e])
        sig = 0.5 * jnp.tanh(0.5 * gate_pre) + 0.5
        act = gate_pre * sig
        hid[...] = (act * up_pre).astype(jnp.bfloat16)
        both[:, :units] = (d_hidden * up_pre * (sig + act * (1.0 - sig))).astype(jnp.bfloat16)
        both[:, units:] = (d_hidden * act).astype(jnp.bfloat16)
        x_part = x_rows[e, :, pl.ds(pl.multiple_of(shard * x_cut, LANES), x_cut)]
        h_part = hid[:, pl.ds(pl.multiple_of(shard * h_cut, LANES), h_cut)]
        grad_both = contract_first(x_part, both[...])
        grads = [grad_both[:, :units], grad_both[:, units:], contract_first(h_part, d_out)]
        for m in range(3):
            grad = grads[m] if first else acc_refs[m][e] + grads[m]
            if last:
                final_buf[m][e] = grad.astype(jnp.bfloat16)
                grad_out(e, m).start()
            else:
                out_refs[m][e] = grad
        if own:
            kept = own * depth
            back[e] = (
                contract_last(both[:kept, :units], gate_ref[e])
                + contract_last(both[:kept, units:], up_ref[e])
            ).astype(jnp.bfloat16)
        return 0

    lax.fori_loop(0, held, expert, 0)

    if own:

        def piece_out(odd, p):
            return pltpu.make_async_copy(
                piece_buf[odd].at[p], piece_hbm[odd].at[p], piece_sem.at[odd, p]
            )

        def collect(p, _):
            for odd in range(2):
                at = pl.ds(pl.multiple_of((2 * p + odd) * depth, depth), depth)
                rows_b = jnp.concatenate([back[i, at, :] for i in range(held)], axis=0)
                piece_buf[odd][p] = contract_first(places[2 * p + odd], rows_b).astype(
                    jnp.bfloat16
                )
                piece_out(odd, p).start()
            return 0

        lax.fori_loop(0, own // 2, collect, 0)
        for p in range(own // 2):
            for odd in range(2):
                piece_out(odd, p).wait()
    if last:
        for e in range(held):
            for m in range(3):
                grad_out(e, m).wait()


def group(records, weights, accs, shards, depth, last=False, own=0):
    tok_dev, record = records[0].shape
    held, width, units = weights[0].shape
    blocks = len(records)
    rows = blocks * depth
    first = accs is None
    grad_shapes = [
        (held, width // shards, units),
        (held, width // shards, units),
        (held, units // shards, width),
    ]
    args = list(records) + list(weights) + ([] if first else list(accs))
    out_type = jnp.bfloat16 if last else jnp.float32
    holder = jax.ShapeDtypeStruct if last else pltpu.VMEM
    out_shape = [holder(s, out_type) for s in grad_shapes]
    scratch = [
        pltpu.VMEM((blocks, tok_dev, record), jnp.bfloat16),
        pltpu.VMEM((held, rows, width), jnp.bfloat16),
        pltpu.VMEM((held, rows, width), jnp.bfloat16),
        pltpu.VMEM((rows, units), jnp.bfloat16),
        pltpu.VMEM((rows, 2 * units), jnp.bfloat16),
        pltpu.VMEM((tok_dev, tok_dev), jnp.float32),
    ]
    if last:
        scratch += [pltpu.VMEM(s, jnp.bfloat16) for s in grad_shapes]
    if own:
        piece = (own // 2, tok_dev, width)
        out_shape += [jax.ShapeDtypeStruct(piece, jnp.bfloat16)] * 2
        scratch += [
            pltpu.VMEM((held, own * depth, width), jnp.bfloat16),
            pltpu.VMEM((own, held * depth, tok_dev), jnp.bfloat16),
            pltpu.VMEM(piece, jnp.bfloat16),
            pltpu.VMEM(piece, jnp.bfloat16),
        ]
    scratch += [
        pltpu.SemaphoreType.DMA((blocks,)),
        pltpu.SemaphoreType.DMA((3, held)),
        pltpu.SemaphoreType.DMA((2, max(own // 2, 1))),
    ]
    outside = pl.BlockSpec(memory_space=pltpu.HBM)
    inside = pl.BlockSpec(memory_space=pltpu.VMEM)
    work = 2 * rows * held * width * units
    return pl.pallas_call(
        functools.partial(group_kernel, first, last, own, depth, blocks),
        in_specs=[outside] * blocks + [inside] * (len(args) - blocks),
        out_specs=[outside if last else inside] * 3 + [outside] * (len(out_shape) - 3),
        input_output_aliases={} if first or last else {blocks + 3 + m: m for m in range(3)},
        out_shape=out_shape,
        scratch_shapes=scratch,
        compiler_params=pltpu.CompilerParams(vmem_limit_bytes=VMEM_BYTES),
        cost_estimate=pl.CostEstimate(
            flops=work // 8,
            bytes_accessed=tok_dev * record * 2,
            transcendentals=rows * held * units,
        ),
    )(*args)


def hold_kernel(gate_hbm, up_hbm, down_hbm, gate_ref, up_ref, across_ref, down_buf, sem):
    held, units, _ = down_buf.shape
    refs = ((down_hbm, down_buf), (gate_hbm, gate_ref), (up_hbm, up_ref))
    copies = [pltpu.make_async_copy(a, b, sem.at[m]) for m, (a, b) in enumerate(refs)]
    for copy in copies:
        copy.start()
    copies[0].wait()

    def turn(e, _):
        for at in range(0, units, LANES):
            cut = slice(at, at + LANES)
            across_ref[e, :, cut] = down_buf[e, cut, :].T
        return 0

    lax.fori_loop(0, held, turn, 0)
    for copy in copies[1:]:
        copy.wait()


def hold(w_gate, w_up, w_down):
    held, units, width = w_down.shape
    shapes = [w_gate.shape, w_up.shape, (held, width, units)]
    return pl.pallas_call(
        hold_kernel,
        in_specs=[pl.BlockSpec(memory_space=pl.ANY)] * 3,
        out_specs=[pl.BlockSpec(memory_space=pltpu.VMEM)] * 3,
        out_shape=[pltpu.VMEM(s, w_down.dtype) for s in shapes],
        scratch_shapes=[pltpu.VMEM(w_down.shape, w_down.dtype), pltpu.SemaphoreType.DMA((3,))],
        compiler_params=pltpu.CompilerParams(vmem_limit_bytes=2 * VMEM_BYTES),
        cost_estimate=pl.CostEstimate(flops=0, bytes_accessed=2 * 10**6, transcendentals=0),
    )(w_gate, w_up, w_down)


def choose_kernel(inner_ref, outer_ref, out_ref, buf, sem):
    place = lax.axis_index("dp")
    inner = jnp.logical_and(place > 0, place < lax.axis_size("dp") - 1)

    def move(source, target):
        copy = pltpu.make_async_copy(source, target, sem)
        copy.start()
        copy.wait()

    @pl.when(inner)
    def _():
        move(inner_ref, buf)

    @pl.when(jnp.logical_not(inner))
    def _():
        move(outer_ref, buf)

    move(buf, out_ref)


def choose(inner, outer):
    return pl.pallas_call(
        choose_kernel,
        in_specs=[pl.BlockSpec(memory_space=pl.ANY)] * 2,
        out_specs=pl.BlockSpec(memory_space=pltpu.HBM),
        out_shape=pltpu.HBM(inner.shape, inner.dtype),
        scratch_shapes=[pltpu.VMEM(inner.shape, inner.dtype), pltpu.SemaphoreType.DMA],
        compiler_params=pltpu.CompilerParams(vmem_limit_bytes=VMEM_BYTES),
        cost_estimate=pl.CostEstimate(flops=0, bytes_accessed=10**6, transcendentals=0),
    )(inner, outer)


def swap(value, axis, bit):
    size = lax.axis_size(axis)
    return lax.ppermute(value, axis, [(i, i ^ bit) for i in range(size)])


def beside(value):
    return swap(value, "expert", 2)


def below(value):
    return swap(value, "expert", 4)


def pairs(*blocks):
    return [piece for block in blocks for piece in (block, swap(block, "expert", 1))]


def middle(value):
    return lax.ppermute(value, "dp", [(1, 2), (2, 1)])


def outward(value):
    return lax.ppermute(value, "dp", [(1, 0), (2, 3)])


def gathered_shards(tokens, grad_out, routes, combine, w_gate, w_up, w_down):
    shards = lax.axis_size("dp")
    tok_dev = tokens.shape[0]
    depth = depth_of(tok_dev, routes.shape[1], w_gate.shape[0] * lax.axis_size("expert"))
    tie = lax.optimization_barrier
    o0 = pack(tokens, grad_out, routes, combine)
    x0, y0, o1, near = beside(o0), below(o0), swap(o0, "dp", 1), middle(o0)
    group0 = pairs(o0)
    weights = hold(*tie((w_gate, w_up, w_down, o0))[:3])
    run = functools.partial(group, weights=weights, shards=shards, depth=depth)
    *accs, mine, theirs = run(group0, accs=None, own=2)
    x0, y0, o1, near, accs, theirs = tie((x0, y0, o1, near, accs, theirs))
    near_end, far, d0, x1 = outward(near), middle(o1), below(x0), beside(o1)
    group0 = pairs(x0, y0, o1)
    y0, near, group0, accs = tie((y0, near, group0, accs))
    *accs, even0, odd0 = run(group0, accs=accs, own=4)
    near_end, near, even0, odd0 = tie((near_end, near, even0, odd0))
    o2 = choose(near, near_end)
    far, d0, x1, o2, y0, odd0 = tie((far, d0, x1, o2, y0, odd0))
    x2, y2, far_end = beside(o2), below(o2), outward(far)
    crossed0 = swap(odd0, "expert", 1)
    group1 = pairs(d0, x1, o2)
    pair0 = (even0.astype(jnp.float32) + crossed0.astype(jnp.float32)).astype(jnp.bfloat16)
    group1, pair0, d0 = tie((group1, pair0, d0))
    sent = [beside(pair0[0]), below(pair0[1])]
    *accs, even1, odd1 = run(group1, accs=accs, own=2)
    far_end, far, even1, odd1 = tie((far_end, far, even1, odd1))
    o3 = choose(far, far_end)
    x2, y2, y0, o3, d0, odd1, sent = tie((x2, y2, y0, o3, d0, odd1, sent))
    x3, y3, y1 = beside(o3), below(o3), swap(y0, "dp", 1)
    crossed1 = swap(odd1, "expert", 1)
    group2 = pairs(x2, y2, o3)
    group2, crossed1 = tie((group2, crossed1))
    pair1 = (even1.astype(jnp.float32) + crossed1.astype(jnp.float32)).astype(jnp.bfloat16)
    accs = run(group2, accs=accs)
    x3, y3, accs, pair1, d0, x2 = tie((x3, y3, accs, pair1, d0, x2))
    d3, d2, d1 = beside(y3), below(x2), swap(d0, "dp", 1)
    accs = run(pairs(x3, y3, y1), accs=accs)
    d3, d2, d1, accs, pair1, theirs = tie((d3, d2, d1, accs, pair1, theirs))
    sent += [swap(pair1[0], "expert", 6), swap(theirs[0], "expert", 1)]
    accs = run(pairs(d1, d2, d3), accs=accs, last=True)
    sent, accs = tie((sent, accs))
    total = mine[0].astype(jnp.float32)
    for piece in sent:
        total = total + piece.astype(jnp.float32)
    return (total.astype(jnp.bfloat16), *accs)


def solution(mesh):
    shards, peers = mesh.shape["dp"], mesh.shape["expert"]

    def body(tokens, grad_out, routes, combine, w_gate, w_up, w_down):
        tok_dev, width = tokens.shape
        gathered = shards * peers * tok_dev * (2 * width + tok_dev) * 2
        fits = (
            peers == 8
            and shards == 4
            and peers * w_gate.shape[0] <= tok_dev // 2
            and tok_dev == LANES
            and gathered <= GATHER_BYTES
        )
        plan = gathered_shards if fits else routed_shards
        return plan(tokens, grad_out, routes, combine, w_gate, w_up, w_down)

    return jax.shard_map(
        body,
        mesh=mesh,
        in_specs=(
            P(("dp", "expert"), None),
            P(("dp", "expert"), None),
            P(("dp", "expert"), None),
            P(("dp", "expert"), None),
            P("expert", None, None),
            P("expert", None, None),
            P("expert", None, None),
        ),
        out_specs=(
            P(("dp", "expert"), None),
            P("expert", "dp", None),
            P("expert", "dp", None),
            P("expert", "dp", None),
        ),
        check_vma=False,
    )
```

```python
import functools
import jax
import jax.numpy as jnp
from jax import lax
from jax.experimental import pallas as pl
from jax.experimental.pallas import tpu as pltpu
from jax.sharding import PartitionSpec as P

LANES = 128
VMEM_BYTES = 26 * 1024 * 1024
GATHER_BYTES = 48 * 1024 * 1024


def slot_ranks(route_block, expert_total):
    flat_ids = route_block.reshape(-1)
    marks = (flat_ids[:, None] == jnp.arange(expert_total, dtype=jnp.int32)[None, :]).astype(
        jnp.int32
    )
    return jnp.sum((jnp.cumsum(marks, axis=0) - 1) * marks, axis=1)


def build_slots(route_block, expert_total, slot_depth):
    flat_ids = route_block.reshape(-1)
    pair_total = flat_ids.shape[0]
    slot_rank = slot_ranks(route_block, expert_total)
    slots = jnp.full((expert_total, slot_depth), pair_total, dtype=jnp.int32)
    slots = slots.at[flat_ids, slot_rank].set(jnp.arange(pair_total, dtype=jnp.int32))
    return (slots, slot_rank)


def contract_last(left, right):
    return lax.dot_general(
        left, right, (((1,), (1,)), ((), ())), preferred_element_type=jnp.float32
    )


def contract_first(left, right):
    return lax.dot_general(
        left, right, (((0,), (0,)), ((), ())), preferred_element_type=jnp.float32
    )


def mul(left, right):
    return jnp.dot(left, right, preferred_element_type=jnp.float32)


def depth_of(tok_dev, top_count, expert_total):
    return 8 * ((tok_dev * top_count * 6 // (5 * expert_total) + 7) // 8)


def expert_backward(rows_x, rows_dy, rows_c, gate_w, up_w, down_w):
    gate_pre = mul(rows_x, gate_w)
    up_pre = mul(rows_x, up_w)
    sigmoid_gate = jax.nn.sigmoid(gate_pre)
    hidden = (gate_pre * sigmoid_gate * up_pre).astype(jnp.bfloat16)
    d_out = (rows_c[:, None] * rows_dy.astype(jnp.float32)).astype(jnp.bfloat16)
    d_hidden = contract_last(d_out, down_w)
    d_gate = (d_hidden * up_pre * sigmoid_gate * (1.0 + gate_pre * (1.0 - sigmoid_gate))).astype(
        jnp.bfloat16
    )
    d_up = (d_hidden * gate_pre * sigmoid_gate).astype(jnp.bfloat16)
    d_rows = (contract_last(d_gate, gate_w) + contract_last(d_up, up_w)).astype(jnp.bfloat16)
    return (hidden, d_out, d_gate, d_up, d_rows)


def routed_shards(tokens, grad_out, routes, combine, w_gate, w_up, w_down):
    tok_dev, model_width = tokens.shape
    top_count = routes.shape[1]
    peer_count = lax.axis_size("expert")
    held_experts = w_gate.shape[0]
    hidden_units = w_gate.shape[2]
    expert_total = peer_count * held_experts
    slot_depth = depth_of(tok_dev, top_count, expert_total)
    pair_total = tok_dev * top_count
    slots, slot_rank = build_slots(routes, expert_total, slot_depth)
    filled = slots < pair_total
    token_index = jnp.where(filled, slots // top_count, tok_dev)
    pad_row = jnp.zeros((1, model_width), jnp.bfloat16)
    send_x = jnp.concatenate([tokens, pad_row])[token_index].reshape(
        peer_count, held_experts, slot_depth, model_width
    )
    send_dy = jnp.concatenate([grad_out, pad_row])[token_index].reshape(
        peer_count, held_experts, slot_depth, model_width
    )
    weight_ext = jnp.concatenate([combine.reshape(-1), jnp.zeros((1,), jnp.bfloat16)])
    send_c = weight_ext[slots].reshape(peer_count, held_experts, slot_depth)
    recv_x, recv_dy, recv_c = (
        lax.all_to_all(send_x, "expert", split_axis=0, concat_axis=0, tiled=True),
        lax.all_to_all(send_dy, "expert", split_axis=0, concat_axis=0, tiled=True),
        lax.all_to_all(send_c, "expert", split_axis=0, concat_axis=0, tiled=True),
    )
    gate_parts = []
    up_parts = []
    down_parts = []
    row_list = []
    for which in range(held_experts):
        rows_x = recv_x[:, which].reshape(-1, model_width)
        rows_dy = recv_dy[:, which].reshape(-1, model_width)
        rows_c = recv_c[:, which].reshape(-1).astype(jnp.float32)
        hidden, d_out, d_gate, d_up, d_rows = expert_backward(
            rows_x, rows_dy, rows_c, w_gate[which], w_up[which], w_down[which]
        )
        d_both = jnp.concatenate([d_gate, d_up], axis=1)
        row_list.append(d_rows.reshape(peer_count, slot_depth, model_width))
        summed = lax.psum_scatter(
            contract_first(rows_x, d_both).astype(jnp.bfloat16),
            "dp",
            scatter_dimension=0,
            tiled=True,
        ).astype(jnp.float32)
        gate_parts.append(summed[:, :hidden_units].astype(jnp.bfloat16))
        up_parts.append(summed[:, hidden_units:].astype(jnp.bfloat16))
        down_parts.append(
            lax.psum_scatter(
                contract_first(hidden, d_out).astype(jnp.bfloat16),
                "dp",
                scatter_dimension=0,
                tiled=True,
            )
        )
    grad_gate = jnp.stack(gate_parts)
    grad_up = jnp.stack(up_parts)
    grad_down = jnp.stack(down_parts)
    stacked = jnp.stack(row_list, axis=1)
    returned = lax.all_to_all(stacked, "expert", split_axis=0, concat_axis=0, tiled=True)
    flat_back = returned.reshape(expert_total * slot_depth, model_width)
    row_of_pair = routes.reshape(-1) * slot_depth + slot_rank
    per_pair = flat_back[row_of_pair].astype(jnp.float32).reshape(tok_dev, top_count, model_width)
    grad_tokens = jnp.sum(per_pair, axis=1).astype(jnp.bfloat16)
    return (grad_tokens, grad_gate, grad_up, grad_down)


def pack_kernel(tok_ref, dy_ref, routes_ref, combine_ref, out_ref):
    tok_dev, width = tok_ref.shape
    half = tok_dev // 2
    out_ref[:, :width] = tok_ref[...]
    out_ref[:, width : 2 * width] = dy_ref[...]
    ids = lax.broadcasted_iota(jnp.int32, (half, tok_dev), 0)
    weight = jnp.zeros((half, tok_dev), jnp.float32)
    named = jnp.zeros((half, tok_dev), jnp.float32)
    for k in range(routes_ref.shape[0]):
        hit = routes_ref[k : k + 1, :] == ids
        weight = jnp.where(hit, combine_ref[k : k + 1, :].astype(jnp.float32), weight)
        named = jnp.where(hit, 1.0, named)
    earlier = lax.broadcasted_iota(jnp.int32, (tok_dev, tok_dev), 0) < lax.broadcasted_iota(
        jnp.int32, (tok_dev, tok_dev), 1
    )
    rank = mul(named.astype(jnp.bfloat16), earlier.astype(jnp.bfloat16))
    rank = jnp.where(named > 0.0, rank, -1.0)
    out_ref[:, 2 * width :] = jnp.concatenate([weight, rank], axis=0).astype(jnp.bfloat16)


def pack(tokens, grad_out, routes, combine):
    tok_dev, width = tokens.shape
    return pl.pallas_call(
        pack_kernel,
        out_shape=jax.ShapeDtypeStruct((tok_dev, 2 * width + tok_dev), jnp.bfloat16),
        compiler_params=pltpu.CompilerParams(vmem_limit_bytes=60 * 1024 * 1024),
        cost_estimate=pl.CostEstimate(flops=10**7, bytes_accessed=2 * 10**6, transcendentals=0),
    )(tokens, grad_out, routes.T, combine.T)


def group_kernel(first, last, own, depth, blocks, *refs):
    refs = list(refs)

    def take(count):
        return [refs.pop(0) for _ in range(count)]

    block_hbm = take(blocks)
    gate_ref, up_ref, across_ref = take(3)
    acc_refs = [] if first else take(3)
    out_refs = take(3)
    piece_hbm = take(2) if own else []
    block_buf, x_rows, d_rows, hid, both, info = take(6)
    final_buf = take(3) if last else []
    if own:
        back, places, *piece_buf = take(4)
    block_sem, out_sem, piece_sem = take(3)
    held, rows, width = x_rows.shape
    tok_dev = block_buf.shape[1]
    half = tok_dev // 2
    units = hid.shape[1]
    shard = lax.axis_index("dp")
    base = lax.axis_index("expert") * held
    x_cut = out_refs[0].shape[1]
    h_cut = out_refs[2].shape[1]

    def grad_out(e, m):
        return pltpu.make_async_copy(final_buf[m].at[e], out_refs[m].at[e], out_sem.at[m, e])

    for b in range(blocks):
        pltpu.make_async_copy(block_hbm[b], block_buf.at[b], block_sem.at[b]).start()

    slot = lax.broadcasted_iota(jnp.int32, (depth, tok_dev), 0).astype(jnp.float32)

    def select(b, _):
        pltpu.make_async_copy(block_hbm[0], block_buf.at[b], block_sem.at[b]).wait()
        info[...] = block_buf[b, :, 2 * width :].astype(jnp.float32)
        picks, scaled = [], []
        for i in range(held):
            weight = info[pl.ds(base + i, 1), :]
            rank = info[pl.ds(half + base + i, 1), :]
            hit = slot == rank
            picks.append(jnp.where(hit, 1.0, 0.0))
            scaled.append(jnp.where(hit, weight, 0.0))
        pick = jnp.concatenate(picks, axis=0).astype(jnp.bfloat16)
        scale = jnp.concatenate(scaled, axis=0).astype(jnp.bfloat16)
        if own:

            @pl.when(b < own)
            def _():
                places[b] = pick

        got_x = mul(pick, block_buf[b, :, :width]).astype(jnp.bfloat16)
        got_d = mul(scale, block_buf[b, :, width : 2 * width]).astype(jnp.bfloat16)
        at = pl.ds(pl.multiple_of(b * depth, depth), depth)
        for i in range(held):
            x_rows[i, at, :] = got_x[i * depth : (i + 1) * depth]
            d_rows[i, at, :] = got_d[i * depth : (i + 1) * depth]
        return 0

    lax.fori_loop(0, blocks, select, 0)

    def expert(e, _):
        rows_x = x_rows[e]
        d_out = d_rows[e]
        step = min(units, 256)
        for at in range(0, units, step):
            cut = slice(at, at + step)
            gate_pre = mul(rows_x, gate_ref[e, :, cut])
            up_pre = mul(rows_x, up_ref[e, :, cut])
            d_hidden = mul(d_out, across_ref[e, :, cut])
            sig = 0.5 * jnp.tanh(0.5 * gate_pre) + 0.5
            act = gate_pre * sig
            hid[:, cut] = (act * up_pre).astype(jnp.bfloat16)
            both[:, cut] = (d_hidden * up_pre * (sig + act * (1.0 - sig))).astype(jnp.bfloat16)
            both[:, units + at : units + at + step] = (d_hidden * act).astype(jnp.bfloat16)
        x_part = x_rows[e, :, pl.ds(pl.multiple_of(shard * x_cut, LANES), x_cut)]
        h_part = hid[:, pl.ds(pl.multiple_of(shard * h_cut, LANES), h_cut)]
        grad_both = contract_first(x_part, both[...])
        grads = [grad_both[:, :units], grad_both[:, units:], contract_first(h_part, d_out)]
        for m in range(3):
            grad = grads[m] if first else acc_refs[m][e] + grads[m]
            if last:
                final_buf[m][e] = grad.astype(jnp.bfloat16)
                grad_out(e, m).start()
            else:
                out_refs[m][e] = grad
        if own:
            kept = own * depth
            back[e] = (
                contract_last(both[:kept, :units], gate_ref[e])
                + contract_last(both[:kept, units:], up_ref[e])
            ).astype(jnp.bfloat16)
        return 0

    lax.fori_loop(0, held, expert, 0)

    if own:

        def piece_out(odd, p):
            return pltpu.make_async_copy(
                piece_buf[odd].at[p], piece_hbm[odd].at[p], piece_sem.at[odd, p]
            )

        def collect(p, _):
            for odd in range(2):
                at = pl.ds(pl.multiple_of((2 * p + odd) * depth, depth), depth)
                rows_b = jnp.concatenate([back[i, at, :] for i in range(held)], axis=0)
                piece_buf[odd][p] = contract_first(places[2 * p + odd], rows_b).astype(
                    jnp.bfloat16
                )
                piece_out(odd, p).start()
            return 0

        lax.fori_loop(0, own // 2, collect, 0)
        for p in range(own // 2):
            for odd in range(2):
                piece_out(odd, p).wait()
    if last:
        for e in range(held):
            for m in range(3):
                grad_out(e, m).wait()


def group(records, weights, accs, shards, depth, last=False, own=0):
    tok_dev, record = records[0].shape
    held, width, units = weights[0].shape
    blocks = len(records)
    rows = blocks * depth
    first = accs is None
    grad_shapes = [
        (held, width // shards, units),
        (held, width // shards, units),
        (held, units // shards, width),
    ]
    args = list(records) + list(weights) + ([] if first else list(accs))
    out_type = jnp.bfloat16 if last else jnp.float32
    holder = jax.ShapeDtypeStruct if last else pltpu.VMEM
    out_shape = [holder(s, out_type) for s in grad_shapes]
    scratch = [
        pltpu.VMEM((blocks, tok_dev, record), jnp.bfloat16),
        pltpu.VMEM((held, rows, width), jnp.bfloat16),
        pltpu.VMEM((held, rows, width), jnp.bfloat16),
        pltpu.VMEM((rows, units), jnp.bfloat16),
        pltpu.VMEM((rows, 2 * units), jnp.bfloat16),
        pltpu.VMEM((tok_dev, tok_dev), jnp.float32),
    ]
    if last:
        scratch += [pltpu.VMEM(s, jnp.bfloat16) for s in grad_shapes]
    if own:
        piece = (own // 2, tok_dev, width)
        out_shape += [jax.ShapeDtypeStruct(piece, jnp.bfloat16)] * 2
        scratch += [
            pltpu.VMEM((held, own * depth, width), jnp.bfloat16),
            pltpu.VMEM((own, held * depth, tok_dev), jnp.bfloat16),
            pltpu.VMEM(piece, jnp.bfloat16),
            pltpu.VMEM(piece, jnp.bfloat16),
        ]
    scratch += [
        pltpu.SemaphoreType.DMA((blocks,)),
        pltpu.SemaphoreType.DMA((3, held)),
        pltpu.SemaphoreType.DMA((2, max(own // 2, 1))),
    ]
    outside = pl.BlockSpec(memory_space=pltpu.HBM)
    inside = pl.BlockSpec(memory_space=pltpu.VMEM)
    work = 2 * rows * held * width * units
    return pl.pallas_call(
        functools.partial(group_kernel, first, last, own, depth, blocks),
        in_specs=[outside] * blocks + [inside] * (len(args) - blocks),
        out_specs=[outside if last else inside] * 3 + [outside] * (len(out_shape) - 3),
        input_output_aliases={} if first or last else {blocks + 3 + m: m for m in range(3)},
        out_shape=out_shape,
        scratch_shapes=scratch,
        compiler_params=pltpu.CompilerParams(vmem_limit_bytes=VMEM_BYTES),
        cost_estimate=pl.CostEstimate(
            flops=work // 8,
            bytes_accessed=tok_dev * record * 2,
            transcendentals=rows * held * units,
        ),
    )(*args)


def hold_kernel(gate_hbm, up_hbm, down_hbm, gate_ref, up_ref, across_ref, down_buf, sem):
    held, units, _ = down_buf.shape
    refs = ((down_hbm, down_buf), (gate_hbm, gate_ref), (up_hbm, up_ref))
    copies = [pltpu.make_async_copy(a, b, sem.at[m]) for m, (a, b) in enumerate(refs)]
    for copy in copies:
        copy.start()
    copies[0].wait()

    def turn(e, _):
        for at in range(0, units, LANES):
            cut = slice(at, at + LANES)
            across_ref[e, :, cut] = down_buf[e, cut, :].T
        return 0

    lax.fori_loop(0, held, turn, 0)
    for copy in copies[1:]:
        copy.wait()


def hold(w_gate, w_up, w_down):
    held, units, width = w_down.shape
    shapes = [w_gate.shape, w_up.shape, (held, width, units)]
    return pl.pallas_call(
        hold_kernel,
        in_specs=[pl.BlockSpec(memory_space=pl.ANY)] * 3,
        out_specs=[pl.BlockSpec(memory_space=pltpu.VMEM)] * 3,
        out_shape=[pltpu.VMEM(s, w_down.dtype) for s in shapes],
        scratch_shapes=[pltpu.VMEM(w_down.shape, w_down.dtype), pltpu.SemaphoreType.DMA((3,))],
        compiler_params=pltpu.CompilerParams(vmem_limit_bytes=2 * VMEM_BYTES),
        cost_estimate=pl.CostEstimate(flops=0, bytes_accessed=2 * 10**6, transcendentals=0),
    )(w_gate, w_up, w_down)


def choose_kernel(inner_ref, outer_ref, out_ref, buf, sem):
    place = lax.axis_index("dp")
    inner = jnp.logical_and(place > 0, place < lax.axis_size("dp") - 1)

    def move(source, target):
        copy = pltpu.make_async_copy(source, target, sem)
        copy.start()
        copy.wait()

    @pl.when(inner)
    def _():
        move(inner_ref, buf)

    @pl.when(jnp.logical_not(inner))
    def _():
        move(outer_ref, buf)

    move(buf, out_ref)


def choose(inner, outer):
    return pl.pallas_call(
        choose_kernel,
        in_specs=[pl.BlockSpec(memory_space=pl.ANY)] * 2,
        out_specs=pl.BlockSpec(memory_space=pltpu.HBM),
        out_shape=pltpu.HBM(inner.shape, inner.dtype),
        scratch_shapes=[pltpu.VMEM(inner.shape, inner.dtype), pltpu.SemaphoreType.DMA],
        compiler_params=pltpu.CompilerParams(vmem_limit_bytes=VMEM_BYTES),
        cost_estimate=pl.CostEstimate(flops=0, bytes_accessed=10**6, transcendentals=0),
    )(inner, outer)


def swap(value, axis, bit):
    size = lax.axis_size(axis)
    return lax.ppermute(value, axis, [(i, i ^ bit) for i in range(size)])


def beside(value):
    return swap(value, "expert", 2)


def below(value):
    return swap(value, "expert", 4)


def pairs(*blocks):
    return [piece for block in blocks for piece in (block, swap(block, "expert", 1))]


def middle(value):
    return lax.ppermute(value, "dp", [(1, 2), (2, 1)])


def outward(value):
    return lax.ppermute(value, "dp", [(1, 0), (2, 3)])


def gathered_shards(tokens, grad_out, routes, combine, w_gate, w_up, w_down):
    shards = lax.axis_size("dp")
    tok_dev = tokens.shape[0]
    depth = depth_of(tok_dev, routes.shape[1], w_gate.shape[0] * lax.axis_size("expert"))
    tie = lax.optimization_barrier
    o0 = pack(tokens, grad_out, routes, combine)
    x0, y0, o1, near = beside(o0), below(o0), swap(o0, "dp", 1), middle(o0)
    group0 = pairs(o0)
    weights = hold(*tie((w_gate, w_up, w_down, o0))[:3])
    run = functools.partial(group, weights=weights, shards=shards, depth=depth)
    *accs, mine, theirs = run(group0, accs=None, own=2)
    x0, y0, o1, near, accs, theirs = tie((x0, y0, o1, near, accs, theirs))
    near_end, far, d0, x1 = outward(near), middle(o1), below(x0), beside(o1)
    group0 = pairs(x0, y0, o1)
    y0, near, group0, accs = tie((y0, near, group0, accs))
    *accs, even0, odd0 = run(group0, accs=accs, own=4)
    near_end, near, even0, odd0 = tie((near_end, near, even0, odd0))
    o2 = choose(near, near_end)
    far, d0, x1, o2, y0, odd0 = tie((far, d0, x1, o2, y0, odd0))
    x2, y2, far_end = beside(o2), below(o2), outward(far)
    crossed0 = swap(odd0, "expert", 1)
    group1 = pairs(d0, x1, o2)
    pair0 = (even0.astype(jnp.float32) + crossed0.astype(jnp.float32)).astype(jnp.bfloat16)
    group1, pair0, d0 = tie((group1, pair0, d0))
    sent = [beside(pair0[0]), below(pair0[1])]
    *accs, even1, odd1 = run(group1, accs=accs, own=2)
    far_end, far, even1, odd1 = tie((far_end, far, even1, odd1))
    o3 = choose(far, far_end)
    x2, y2, y0, o3, d0, odd1, sent = tie((x2, y2, y0, o3, d0, odd1, sent))
    x3, y3, y1 = beside(o3), below(o3), swap(y0, "dp", 1)
    crossed1 = swap(odd1, "expert", 1)
    group2 = pairs(x2, y2, o3)
    group2, crossed1 = tie((group2, crossed1))
    pair1 = (even1.astype(jnp.float32) + crossed1.astype(jnp.float32)).astype(jnp.bfloat16)
    accs = run(group2, accs=accs)
    x3, y3, accs, pair1, d0, x2 = tie((x3, y3, accs, pair1, d0, x2))
    d3, d2, d1 = beside(y3), below(x2), swap(d0, "dp", 1)
    accs = run(pairs(x3, y3, y1), accs=accs)
    d3, d2, d1, accs, pair1, theirs = tie((d3, d2, d1, accs, pair1, theirs))
    sent += [swap(pair1[0], "expert", 6), swap(theirs[0], "expert", 1)]
    accs = run(pairs(d1, d2, d3), accs=accs, last=True)
    sent, accs = tie((sent, accs))
    total = mine[0].astype(jnp.float32)
    for piece in sent:
        total = total + piece.astype(jnp.float32)
    return (total.astype(jnp.bfloat16), *accs)


def solution(mesh):
    shards, peers = mesh.shape["dp"], mesh.shape["expert"]

    def body(tokens, grad_out, routes, combine, w_gate, w_up, w_down):
        tok_dev, width = tokens.shape
        gathered = shards * peers * tok_dev * (2 * width + tok_dev) * 2
        fits = (
            peers == 8
            and shards == 4
            and peers * w_gate.shape[0] <= tok_dev // 2
            and tok_dev == LANES
            and gathered <= GATHER_BYTES
        )
        plan = gathered_shards if fits else routed_shards
        return plan(tokens, grad_out, routes, combine, w_gate, w_up, w_down)

    return jax.shard_map(
        body,
        mesh=mesh,
        in_specs=(
            P(("dp", "expert"), None),
            P(("dp", "expert"), None),
            P(("dp", "expert"), None),
            P(("dp", "expert"), None),
            P("expert", None, None),
            P("expert", None, None),
            P("expert", None, None),
        ),
        out_specs=(
            P(("dp", "expert"), None),
            P("expert", "dp", None),
            P("expert", "dp", None),
            P("expert", "dp", None),
        ),
        check_vma=False,
    )
```
